32 devices in a mesh: groups: 2 (over y), row: 8 (over z, core), col: 2 (over x).
Axes of the slice: x: 2, y: 2, z: 4, core: 2. Of those that a mesh axis runs over, the one named last changes fastest.
Arguments:
- pair_rep: bfloat16 [192, 96, 128], P(('groups', 'row'), 'col'), parts along dimension 0, may hold values from -6 to 6
- token_mask: int32 [192], P('groups'), parts along dimension 0, may hold values 0 or 1
- out_project: bfloat16 [128, 512], replicated, may hold values from -0.5 to 0.5
- out_gating: bfloat16 [128, 128], replicated, may hold values from -0.5 to 0.5
- out_final: bfloat16 [128, 128], replicated, may hold values from -0.5 to 0.5
- in_project: bfloat16 [128, 512], replicated, may hold values from -0.5 to 0.5
- in_gating: bfloat16 [128, 128], replicated, may hold values from -0.5 to 0.5
- in_final: bfloat16 [128, 128], replicated, may hold values from -0.5 to 0.5
Outputs:
- updated_pair: bfloat16 [192, 96, 128], P(('groups', 'row'), 'col'), parts along dimension 0
The draws below stay inside these ranges and needn't reach their ends.
There are 2 independent parts, one for each index of `groups`. The reference program is written for one: setup_inputs(seed, part) draws one part's arguments, and reference() takes and returns one part's arrays. A program takes and returns all parts, laid end to end along the dimension named above; an argument that names none is the same for every part. Nothing has to cross between parts.
All inputs are finite; a program needn't handle non-finite values.
Results may differ from the reference program's by a relative error of at most 0.012.
Values may be sent and summed in bfloat16 or wider, within the bound.
No kernel may reach another device: no remote copies, remote signals or barrier semaphores. Data moves between devices by JAX's collectives and lax.ppermute only.
A program may use at most 64 MiB of HBM per device.

```python
import jax
import jax.numpy as jnp
from jax import lax

C = 128
HID = 128
TOKENS = 96


def plant(result, stream_key, low, high):
    longest = result.shape.index(max(result.shape))
    spots = []
    for shift in (0, 1):
        where = [jax.random.randint(jax.random.fold_in(stream_key, axis), (), 0, length) for axis, length in enumerate(result.shape)]
        where[longest] = (where[longest] + shift) % result.shape[longest]
        spots.append(tuple(where))
    return result.at[spots[0]].set(low).at[spots[1]].set(high)


def steps_of(own_key, dims, shards, low, high):
    loudness, own = 1.0, jax.random.fold_in(own_key, 6)
    for position, blocks in shards:
        draws = jnp.exp(jax.random.uniform(jax.random.fold_in(own, position), (blocks,), jnp.float32, low / len(shards), high / len(shards)))
        loudness = loudness * jnp.repeat(draws, dims[position] // blocks).reshape([-1 if axis == position else 1 for axis in range(len(dims))])
    return loudness


def centred(stream_key, shape, scale, limit, pieces=(), dtype=jnp.bfloat16):
    drawn = jax.random.normal(stream_key, shape, jnp.float32) * scale
    if len(pieces) > 0:
        drawn = steps_of(stream_key, shape, pieces, -0.22, 0.18) * drawn
    return jnp.clip(drawn, min=-limit, max=limit).astype(dtype)


def setup_inputs(seed: int = 0, part: int = 0) -> dict:
    key_of = jax.random.split(jax.random.key(seed), 9)
    own_keys = jax.random.split(jax.random.fold_in(key_of[8], part), 9)
    return {
        "pair_rep": centred(own_keys[0], (TOKENS, TOKENS, C), 1.0, 6.0, ((0, 8), (1, 2))),
        "token_mask": plant((jax.random.randint(own_keys[1], (TOKENS,), 0, 8) < 7).astype(jnp.int32), jax.random.fold_in(own_keys[1], 1), 0, 1),
        "out_project": centred(key_of[2], (C, 4 * HID), C ** -0.5, 0.5),
        "out_gating": centred(key_of[3], (C, C), C ** -0.5, 0.5),
        "out_final": centred(key_of[4], (HID, C), HID ** -0.5, 0.5),
        "in_project": centred(key_of[5], (C, 4 * HID), C ** -0.5, 0.5),
        "in_gating": centred(key_of[6], (C, C), C ** -0.5, 0.5),
        "in_final": centred(key_of[7], (HID, C), HID ** -0.5, 0.5),
    }


def layer_norm(values):
    center = lax.optimization_barrier(jnp.mean(values, axis=-1, keepdims=True))
    spread = lax.optimization_barrier(jnp.mean((values - center) ** 2, axis=-1, keepdims=True))
    return (values - center) / jnp.sqrt(spread + 1e-05)

def triangle_update(pair_block, token_mask, w_project, w_gating, w_final, outgoing):
    normed = layer_norm(pair_block.astype(jnp.float32)).astype(jnp.bfloat16)
    projected = jnp.dot(normed, w_project, preferred_element_type=jnp.float32)
    weight_mask = token_mask.astype(jnp.float32)
    pair_mask = (weight_mask[:, None] * weight_mask[None, :])[:, :, None]
    left_proj = (pair_mask * jax.nn.sigmoid(projected[..., HID:2 * HID]) * projected[..., :HID]).astype(jnp.bfloat16)
    right_proj = (pair_mask * jax.nn.sigmoid(projected[..., 3 * HID:]) * projected[..., 2 * HID:3 * HID]).astype(jnp.bfloat16)
    gate_value = jax.nn.sigmoid(jnp.dot(normed, w_gating, preferred_element_type=jnp.float32))
    if outgoing:
        product = jnp.einsum('ikc,jkc->ijc', left_proj.astype(jnp.float32), right_proj.astype(jnp.float32))
    else:
        product = jnp.einsum('kic,kjc->ijc', left_proj.astype(jnp.float32), right_proj.astype(jnp.float32))
    mixed_rows = layer_norm(product).astype(jnp.bfloat16)
    return pair_block.astype(jnp.float32) + gate_value * jnp.dot(mixed_rows, w_final, preferred_element_type=jnp.float32)

def reference(pair_rep, token_mask, out_project, out_gating, out_final, in_project, in_gating, in_final):
    first_pass = triangle_update(pair_rep, token_mask, out_project, out_gating, out_final, True).astype(jnp.bfloat16)
    return triangle_update(first_pass, token_mask, in_project, in_gating, in_final, False).astype(jnp.bfloat16)
```

```python
import functools

import jax
import jax.numpy as jnp
from jax import lax
from jax.experimental import pallas as pl
from jax.experimental.pallas import tpu as pltpu
from jax.sharding import PartitionSpec as P

F32, BF16 = jnp.float32, jnp.bfloat16
VMEM = pl.BlockSpec(memory_space=pltpu.VMEM)
LIMIT = 40 * 1024 * 1024


def call(kernel, outs, args, scratch=(), flops=10_000_000, name=None):
    single = not isinstance(outs, (list, tuple))
    outs = [outs] if single else list(outs)
    moved = sum(a.size * a.dtype.itemsize for a in args) + sum(
        o.size * o.dtype.itemsize for o in outs
    )
    result = pl.pallas_call(
        kernel,
        out_shape=outs,
        in_specs=[VMEM] * len(args),
        out_specs=[VMEM] * len(outs),
        scratch_shapes=list(scratch),
        compiler_params=pltpu.CompilerParams(vmem_limit_bytes=LIMIT),
        cost_estimate=pl.CostEstimate(flops=flops, bytes_accessed=moved, transcendentals=0),
        name=name,
    )(*args)
    return result[0] if single else result


def shape(dims, dtype):
    return jax.ShapeDtypeStruct(dims, dtype)


def sigmoid(v):
    return 0.5 * jnp.tanh(0.5 * v) + 0.5


def layer_norm(v):
    center = jnp.mean(v, axis=-1, keepdims=True)
    shifted = v - center
    spread = jnp.mean(shifted * shifted, axis=-1, keepdims=True)
    return shifted * lax.rsqrt(spread + 1e-05)


def place():
    row = lax.axis_index("row")
    return row // 2, row % 2, lax.axis_index("col")


def token_weights(mask_row, start, count):
    tokens = mask_row.shape[1]
    lane = lax.broadcasted_iota(jnp.int32, (count, tokens), 1)
    row = lax.broadcasted_iota(jnp.int32, (count, tokens), 0)
    hot = jnp.where(lane == row + start, mask_row, 0.0).astype(BF16)
    return jnp.dot(hot, jnp.ones((tokens, 128), BF16), preferred_element_type=F32)


def gated(normed, w, mask_ref, rows, cols):
    hidden = w.shape[1] // 2
    projected = jnp.dot(normed, w, preferred_element_type=F32)
    value = sigmoid(projected[:, hidden:]) * projected[:, :hidden]
    mask_row = mask_ref[...].astype(F32)
    row_w = token_weights(mask_row, lax.axis_index("row") * rows, -(-rows // 8) * 8)
    col_w = token_weights(mask_row, lax.axis_index("col") * cols, cols)
    weights = row_w[:rows, None, :] * col_w[None, :, :]
    return value * weights.reshape(rows * cols, 128)


def right_kernel(half, pair_ref, mask_ref, w_ref, right_ref):
    rows, cols, chan = pair_ref.shape
    normed = layer_norm(pair_ref[...].astype(F32)).astype(BF16).reshape(rows * cols, chan)
    width = w_ref.shape[1] // 2
    w = w_ref[:, half * width : (half + 1) * width]
    value = gated(normed, w, mask_ref, rows, cols)
    right_ref[...] = value.astype(BF16).reshape(right_ref.shape)


def gate_kernel(pair_ref, w_ref, gate_ref):
    rows, cols, chan = pair_ref.shape
    normed = layer_norm(pair_ref[...].astype(F32)).astype(BF16).reshape(rows * cols, chan)
    gate = sigmoid(jnp.dot(normed, w_ref[...], preferred_element_type=F32))
    gate_ref[...] = gate.reshape(gate_ref.shape)


def outgoing_kernel(own_left, core_left, *refs):
    rights, (mine_ref, other_ref, r_scr, l_scr) = refs[:-4], refs[-4:]
    rows, cols, chan = own_left.shape
    count = len(rights)
    width = count * rows
    z, _, _ = place()
    low = z % count
    for m, ref in enumerate(rights):
        base = (low ^ m) * rows
        for j in range(rows):
            r_scr[pl.ds(base + j, cols, stride=width), :] = ref[j].astype(F32)
    for out_ref, left in ((mine_ref, own_left), (other_ref, core_left)):
        l_scr[...] = left[...].astype(F32).reshape(rows * cols, chan)

        def step(block, totals):
            for u in range(8):
                k = block * 8 + u
                right = r_scr[pl.ds(pl.multiple_of(k * width, 8), width), :]
                totals = tuple(
                    t + l_scr[pl.ds(i * cols + k, 1), :] * right for i, t in enumerate(totals)
                )
            return totals

        zero = jnp.zeros((width, chan), F32)
        totals = lax.fori_loop(0, cols // 8, step, (zero,) * rows)
        for i, t in enumerate(totals):
            out_ref[i] = t.astype(out_ref.dtype)


def first_kernel(cols_n, *refs):
    own, others = refs[0], refs[1 : 2 * cols_n]
    pair_ref, gate_ref, mask_ref, final_ref, w_ref = refs[2 * cols_n : 2 * cols_n + 5]
    first_ref, mine_ref, other_ref, scr, half_scr = refs[2 * cols_n + 5 :]
    rows, cols, chan = pair_ref.shape
    _, core, _ = place()
    same = own[...].astype(F32)
    for ref in others[: cols_n - 1]:
        same = same + ref[...].astype(F32)
    cross = others[cols_n - 1][...].astype(F32)
    for ref in others[cols_n:]:
        cross = cross + ref[...].astype(F32)
    pieces = cols // (2 * rows)
    for value, side in ((same, core), (cross, 1 - core)):
        half_scr[...] = value.reshape(half_scr.shape)
        for i in range(rows):
            for q in range(pieces):
                part = half_scr[pl.ds((i * pieces + q) * rows, rows), :]
                scr[pl.ds(i * cols + (2 * q + side) * rows, rows), :] = part
    mixed = layer_norm(scr[...]).astype(BF16)
    update = jnp.dot(mixed, final_ref[...], preferred_element_type=F32)
    pair = pair_ref[...].astype(F32).reshape(rows * cols, chan)
    first = (pair + gate_ref[...].reshape(rows * cols, chan) * update).astype(BF16)
    first_ref[...] = first.reshape(first_ref.shape)
    normed = layer_norm(first.astype(F32)).astype(BF16)
    w = w_ref[:, : w_ref.shape[1] // 2]
    scr[...] = gated(normed, w, mask_ref, rows, cols)
    for out_ref, side in ((mine_ref, core), (other_ref, 1 - core)):
        for i in range(rows):
            for q in range(pieces):
                part = scr[pl.ds(i * cols + (2 * q + side) * rows, rows), :]
                half_scr[pl.ds((i * pieces + q) * rows, rows), :] = part
        out_ref[...] = half_scr[...].astype(BF16).reshape(out_ref.shape)


def incoming_kernel(cols_n, steps, *refs):
    own_right, core_right = refs[:2]
    lefts = refs[2 : 2 + 2 * cols_n]
    outs = refs[2 + 2 * cols_n : 2 + 2 * cols_n + len(steps)]
    l_scr, r_scr = refs[-2:]
    rows, cols, chan = own_right.shape
    width = lefts[0].shape[1]
    pieces = width // rows
    z, _, x = place()
    for n, ref in enumerate((own_right, core_right)):
        r_scr[pl.ds(n * rows * cols, rows * cols), :] = ref[...].astype(F32).reshape(-1, chan)
    for n, ref in enumerate(lefts):
        l_scr[pl.ds(n * rows * width, rows * width), :] = ref[...].astype(F32).reshape(-1, chan)
    for m, out_ref in zip(steps, outs):
        target = z ^ m
        base = ((target // pieces) ^ x) * (2 * rows * width) + (target % pieces) * rows
        for group in range(0, rows, 6):

            def step(k, totals):
                right = r_scr[pl.ds(pl.multiple_of(k * cols, 8), cols), :]
                return tuple(
                    t + l_scr[pl.ds(base + k * width + group + i, 1), :] * right
                    for i, t in enumerate(totals)
                )

            zero = jnp.zeros((cols, chan), F32)
            totals = lax.fori_loop(0, 2 * rows, step, (zero,) * 6, unroll=4)
            for i, t in enumerate(totals):
                out_ref[group + i] = t.astype(out_ref.dtype)


def last_kernel(*refs):
    parts, (first_ref, gate_ref, final_ref, out_ref) = refs[:-4], refs[-4:]
    rows, cols, chan = first_ref.shape
    product = parts[0][...].astype(F32)
    for ref in parts[1:]:
        product = product + ref[...].astype(F32)
    mixed = layer_norm(product).astype(BF16).reshape(rows * cols, chan)
    update = jnp.dot(mixed, final_ref[...], preferred_element_type=F32)
    first = first_ref[...].astype(F32).reshape(rows * cols, chan)
    result = first + gate_ref[...].reshape(rows * cols, chan) * update
    out_ref[...] = result.astype(BF16).reshape(out_ref.shape)


def on_device(
    rows_n,
    cols_n,
    pair_rep,
    token_mask,
    out_project,
    out_gating,
    out_final,
    in_project,
    in_gating,
    in_final,
):
    rows, cols, chan = pair_rep.shape
    chips = rows_n // 2
    pieces = cols // (2 * rows)
    mask = token_mask.reshape(1, -1)
    block = shape((rows, cols, chan), BF16)
    block32 = shape((rows, cols, chan), F32)
    half = (rows, pieces * rows, chan)

    def along_row(v, bits):
        return lax.ppermute(v, "row", [(i, i ^ bits) for i in range(rows_n)])

    def shift(v, dx, core):
        pairs = [
            (r * cols_n + c, (r ^ core) * cols_n + (c ^ dx))
            for r in range(rows_n)
            for c in range(cols_n)
        ]
        return lax.ppermute(v, ("row", "col"), pairs)

    z, _, x = place()
    offset = (z // pieces) ^ x

    project = lambda pair, w, half: call(
        functools.partial(right_kernel, half), block, [pair, mask, w], flops=100_000_000
    )
    right = project(pair_rep, out_project, 1)
    rights = [right] + [None] * (chips - 1)
    for m in reversed(range(1, chips)):
        rights[m] = along_row(right, 2 * m)
    left = project(pair_rep, out_project, 0)
    core_left = along_row(left, 1)
    gate = call(gate_kernel, block32, [pair_rep, out_gating], flops=50_000_000)
    mine, other = [], []
    for h in range(cols_n):
        a, b = call(
            outgoing_kernel,
            [shape(half, F32), shape(half, BF16)],
            [left, core_left] + rights[h * pieces : (h + 1) * pieces],
            scratch=[
                pltpu.VMEM((cols * pieces * rows, chan), F32),
                pltpu.VMEM((rows * cols, chan), F32),
            ],
            flops=500_000_000,
        )
        mine.append(a)
        other.append(b)

    def pick(options, dx):
        return lax.select_n(offset ^ dx, *options)

    same = [pick(mine, 0)]
    for dx in range(1, cols_n):
        same.append(shift(pick(mine, dx).astype(BF16), dx, 0))
    cross = [shift(pick(other, dx), dx, 1) for dx in range(cols_n)]
    first, left_mine, left_other = call(
        functools.partial(first_kernel, cols_n),
        [block, shape(half, BF16), shape(half, BF16)],
        same + cross + [pair_rep, gate, mask, out_final, in_project],
        scratch=[
            pltpu.VMEM((rows * cols, chan), F32),
            pltpu.VMEM((rows * pieces * rows, chan), F32),
        ],
        flops=200_000_000,
    )

    lefts = []
    for dx in range(cols_n):
        lefts.append(left_mine if dx == 0 else shift(left_mine, dx, 0))
        lefts.append(shift(left_other, dx, 1))
    right = project(first, in_project, 1)
    core_right = along_row(right, 1)

    def partial_products(steps):
        return call(
            functools.partial(incoming_kernel, cols_n, steps),
            [block32 if m == 0 else block for m in steps],
            [right, core_right] + lefts,
            scratch=[
                pltpu.VMEM((2 * cols_n * rows * pieces * rows, chan), F32),
                pltpu.VMEM((2 * rows * cols, chan), F32),
            ],
            flops=200_000_000 * len(steps),
        )

    far = list(range(pieces, chips))
    parts = [None] * chips
    for m, value in zip(far, partial_products(far)):
        parts[m] = along_row(value, 2 * m)
    near = list(range(1, pieces))
    for m, value in zip(near, partial_products(near)):
        parts[m] = along_row(value, 2 * m)
    parts[0] = partial_products([0])[0]
    gate = call(gate_kernel, block32, [first, in_gating], flops=50_000_000)
    return call(last_kernel, block, parts + [first, gate, in_final], flops=100_000_000)


def solution(mesh):
    return jax.shard_map(
        functools.partial(on_device, mesh.shape["row"], mesh.shape["col"]),
        mesh=mesh,
        in_specs=(P(("groups", "row"), "col", None), P("groups"), P(), P(), P(), P(), P(), P()),
        out_specs=P(("groups", "row"), "col", None),
        check_vma=False,
    )
```

```python
import functools

import jax
import jax.numpy as jnp
from jax import lax
from jax.experimental import pallas as pl
from jax.experimental.pallas import tpu as pltpu
from jax.sharding import PartitionSpec as P

F32, BF16 = jnp.float32, jnp.bfloat16
VMEM = pl.BlockSpec(memory_space=pltpu.VMEM)
LIMIT = 40 * 1024 * 1024


def call(kernel, outs, args, scratch=(), flops=10_000_000, outside=()):
    single = not isinstance(outs, (list, tuple))
    outs = [outs] if single else list(outs)
    moved = sum(a.size * a.dtype.itemsize for a in args) + sum(
        o.size * o.dtype.itemsize for o in outs
    )
    result = pl.pallas_call(
        kernel,
        out_shape=outs,
        in_specs=[
            pl.BlockSpec(memory_space=pl.ANY) if n in outside else VMEM for n in range(len(args))
        ],
        out_specs=[VMEM] * len(outs),
        scratch_shapes=list(scratch),
        compiler_params=pltpu.CompilerParams(vmem_limit_bytes=LIMIT),
        cost_estimate=pl.CostEstimate(flops=flops, bytes_accessed=moved, transcendentals=0),
    )(*args)
    return result[0] if single else result


def shape(dims, dtype):
    return jax.ShapeDtypeStruct(dims, dtype)


def sigmoid(v):
    return 0.5 * jnp.tanh(0.5 * v) + 0.5


def layer_norm(v):
    center = jnp.mean(v, axis=-1, keepdims=True)
    shifted = v - center
    spread = jnp.mean(shifted * shifted, axis=-1, keepdims=True)
    return shifted * lax.rsqrt(spread + 1e-05)


def place():
    row = lax.axis_index("row")
    return row // 2, row % 2, lax.axis_index("col")


def token_weights(mask_row, start, count):
    tokens = mask_row.shape[1]
    lane = lax.broadcasted_iota(jnp.int32, (count, tokens), 1)
    row = lax.broadcasted_iota(jnp.int32, (count, tokens), 0)
    hot = jnp.where(lane == row + start, mask_row, 0.0).astype(BF16)
    return jnp.dot(hot, jnp.ones((tokens, 128), BF16), preferred_element_type=F32)


def gated(normed, w, mask_ref, rows, cols, x):
    hidden = w.shape[1] // 2
    projected = jnp.dot(normed, w, preferred_element_type=F32)
    value = sigmoid(projected[:, hidden:]) * projected[:, :hidden]
    mask_row = mask_ref[...].astype(F32)
    row_w = token_weights(mask_row, lax.axis_index("row") * rows, -(-rows // 8) * 8)
    col_w = token_weights(mask_row, x * cols, cols)
    weights = row_w[:rows, None, :] * col_w[None, :, :]
    return value * weights.reshape(rows * cols, 128)


def normed_of(pair):
    rows, cols, chan = pair.shape
    return layer_norm(pair.astype(F32)).astype(BF16).reshape(rows * cols, chan)


def opening_kernel(pair_hbm, mask_hbm, w_hbm, right_ref, pair_scr, mask_scr, w_scr, sems):
    rows, cols, chan = pair_scr.shape
    width = w_scr.shape[1]
    copies = [
        pltpu.make_async_copy(pair_hbm, pair_scr, sems.at[0]),
        pltpu.make_async_copy(w_hbm.at[:, pl.ds(width, width)], w_scr, sems.at[1]),
        pltpu.make_async_copy(mask_hbm, mask_scr, sems.at[2]),
    ]
    for copy in copies:
        copy.start()
    for copy in copies:
        copy.wait()
    value = gated(
        normed_of(pair_scr[...]), w_scr[...], mask_scr, rows, cols, lax.axis_index("col")
    )
    right_ref[...] = value.astype(BF16).reshape(right_ref.shape)


def left_kernel(pair_ref, mask_ref, w_ref, right_hbm, left_ref):
    del right_hbm
    rows, cols, _ = pair_ref.shape
    w = w_ref[:, : w_ref.shape[1] // 2]
    value = gated(normed_of(pair_ref[...]), w, mask_ref, rows, cols, lax.axis_index("col"))
    left_ref[...] = value.astype(BF16).reshape(left_ref.shape)


def right_kernel(*refs):
    firsts, (mask_ref, w_ref, right_ref, own_ref) = refs[:-4], refs[-4:]
    rows, cols, _ = own_ref.shape
    pieces = cols // (2 * rows)
    z, _, x = place()
    for h, ref in enumerate(firsts):

        @pl.when(((z // pieces) ^ h) == x)
        def _():
            own_ref[...] = ref[...]

    w = w_ref[:, w_ref.shape[1] // 2 :]
    value = gated(normed_of(own_ref[...]), w, mask_ref, rows, cols, x)
    right_ref[...] = value.astype(BF16).reshape(right_ref.shape)


def gates_kernel(cols_n, *refs):
    pairs, w_ref, outs = refs[:cols_n], refs[cols_n], refs[cols_n + 1 :]
    rows, cols, _ = pairs[0].shape
    pieces = cols // (2 * rows)
    z, _, x = place()
    for h in range(cols_n):
        pair_ref, gate_ref = outs[2 * h : 2 * h + 2]
        for dx in range(cols_n):

            @pl.when(((z // pieces) ^ x ^ h) == dx)
            def _():
                pair_ref[...] = pairs[dx][...]

        gate = jnp.dot(normed_of(pair_ref[...]), w_ref[...], preferred_element_type=F32)
        gate_ref[...] = sigmoid(gate).reshape(gate_ref.shape)


def gate_kernel(pair_ref, w_ref, gate_ref):
    gate = jnp.dot(normed_of(pair_ref[...]), w_ref[...], preferred_element_type=F32)
    gate_ref[...] = sigmoid(gate).reshape(gate_ref.shape)


def outgoing_kernel(own_left, core_left, *refs):
    rights, (mine_ref, other_ref, r_scr, l_scr) = refs[:-4], refs[-4:]
    rows, cols, chan = own_left.shape
    count = len(rights)
    width = count * rows
    z, _, _ = place()
    low = z % count
    for m, ref in enumerate(rights):
        base = (low ^ m) * rows
        for j in range(rows):
            r_scr[pl.ds(base + j, cols, stride=width), :] = ref[j].astype(F32)
    for out_ref, left in ((mine_ref, own_left), (other_ref, core_left)):
        l_scr[...] = left[...].astype(F32).reshape(rows * cols, chan)

        def step(block, totals):
            for u in range(8):
                k = block * 8 + u
                right = r_scr[pl.ds(pl.multiple_of(k * width, 8), width), :]
                totals = tuple(
                    t + l_scr[pl.ds(i * cols + k, 1), :] * right for i, t in enumerate(totals)
                )
            return totals

        zero = jnp.zeros((width, chan), F32)
        totals = lax.fori_loop(0, cols // 8, step, (zero,) * rows)
        for i, t in enumerate(totals):
            out_ref[i] = t.astype(out_ref.dtype)


def first_kernel(cols_n, h, *refs):
    parts = refs[: 2 * cols_n]
    pair_ref, gate_ref, mask_ref, final_ref, w_ref = refs[2 * cols_n : 2 * cols_n + 5]
    first_ref, mine_ref, other_ref, scr, half_scr = refs[2 * cols_n + 5 :]
    rows, cols, chan = pair_ref.shape
    pieces = cols // (2 * rows)
    z, core, _ = place()
    for group, side in ((parts[:cols_n], core), (parts[cols_n:], 1 - core)):
        value = group[0][...].astype(F32)
        for ref in group[1:]:
            value = value + ref[...].astype(F32)
        half_scr[...] = value.reshape(half_scr.shape)
        for i in range(rows):
            for q in range(pieces):
                part = half_scr[pl.ds((i * pieces + q) * rows, rows), :]
                scr[pl.ds(i * cols + (2 * q + side) * rows, rows), :] = part
    mixed = layer_norm(scr[...]).astype(BF16)
    update = jnp.dot(mixed, final_ref[...], preferred_element_type=F32)
    pair = pair_ref[...].astype(F32).reshape(rows * cols, chan)
    first = (pair + gate_ref[...].reshape(rows * cols, chan) * update).astype(BF16)
    first_ref[...] = first.reshape(first_ref.shape)
    normed = layer_norm(first.astype(F32)).astype(BF16)
    w = w_ref[:, : w_ref.shape[1] // 2]
    scr[...] = gated(normed, w, mask_ref, rows, cols, (z // pieces) ^ h)
    for out_ref, side in ((mine_ref, core), (other_ref, 1 - core)):
        for i in range(rows):
            for q in range(pieces):
                part = scr[pl.ds(i * cols + (2 * q + side) * rows, rows), :]
                half_scr[pl.ds((i * pieces + q) * rows, rows), :] = part
        out_ref[...] = half_scr[...].astype(BF16).reshape(out_ref.shape)


def incoming_kernel(steps, *refs):
    own_right, core_right = refs[:2]
    count = (len(refs) - 4 - len(steps)) // 2
    lefts = refs[2 : 2 + 2 * count]
    outs = refs[2 + 2 * count : -2]
    l_scr, r_scr = refs[-2:]
    rows, cols, chan = own_right.shape
    width = lefts[0].shape[1]
    pieces = width // rows
    z, _, _ = place()
    for n, ref in enumerate((own_right, core_right)):
        r_scr[pl.ds(n * rows * cols, rows * cols), :] = ref[...].astype(F32).reshape(-1, chan)
    for n, ref in enumerate(lefts):
        l_scr[pl.ds(n * rows * width, rows * width), :] = ref[...].astype(F32).reshape(-1, chan)
    for m, out_ref in zip(steps, outs):
        block = m // pieces - steps[0] // pieces
        base = block * (2 * rows * width) + ((z ^ m) % pieces) * rows
        for group in range(0, rows, 6):

            def step(k, totals):
                right = r_scr[pl.ds(pl.multiple_of(k * cols, 8), cols), :]
                return tuple(
                    t + l_scr[pl.ds(base + k * width + group + i, 1), :] * right
                    for i, t in enumerate(totals)
                )

            zero = jnp.zeros((cols, chan), F32)
            totals = lax.fori_loop(0, 2 * rows, step, (zero,) * 6, unroll=4)
            for i, t in enumerate(totals):
                out_ref[group + i] = t.astype(out_ref.dtype)


def last_kernel(*refs):
    parts, (first_ref, gate_ref, final_ref, out_ref) = refs[:-4], refs[-4:]
    rows, cols, chan = first_ref.shape
    product = parts[0][...].astype(F32)
    for ref in parts[1:]:
        product = product + ref[...].astype(F32)
    mixed = layer_norm(product).astype(BF16).reshape(rows * cols, chan)
    update = jnp.dot(mixed, final_ref[...], preferred_element_type=F32)
    first = first_ref[...].astype(F32).reshape(rows * cols, chan)
    result = first + gate_ref[...].reshape(rows * cols, chan) * update
    out_ref[...] = result.astype(BF16).reshape(out_ref.shape)


def on_device(
    rows_n,
    cols_n,
    pair_rep,
    token_mask,
    out_project,
    out_gating,
    out_final,
    in_project,
    in_gating,
    in_final,
):
    rows, cols, chan = pair_rep.shape
    chips = rows_n // 2
    pieces = cols // (2 * rows)
    mask = token_mask.reshape(1, -1)
    block = shape((rows, cols, chan), BF16)
    block32 = shape((rows, cols, chan), F32)
    half = (rows, pieces * rows, chan)

    def along_row(v, bits):
        return lax.ppermute(v, "row", [(i, i ^ bits) for i in range(rows_n)])

    def shift(v, dx, core):
        pairs = [
            (r * cols_n + c, (r ^ core) * cols_n + (c ^ dx))
            for r in range(rows_n)
            for c in range(cols_n)
        ]
        return lax.ppermute(v, ("row", "col"), pairs)

    right = call(
        opening_kernel,
        block,
        [pair_rep, mask, out_project],
        scratch=[
            pltpu.VMEM(pair_rep.shape, BF16),
            pltpu.VMEM(mask.shape, jnp.int32),
            pltpu.VMEM((chan, out_project.shape[1] // 2), BF16),
            pltpu.SemaphoreType.DMA((3,)),
        ],
        flops=100_000_000,
        outside=(0, 1, 2),
    )
    rights = [right] + [None] * (chips - 1)
    for m in reversed(range(1, chips)):
        rights[m] = along_row(right, 2 * m)
    left = call(
        left_kernel,
        block,
        [pair_rep, mask, out_project, right],
        flops=100_000_000,
        outside=(3,),
    )
    core_left = along_row(left, 1)
    pairs = [pair_rep] + [shift(pair_rep, dx, 0) for dx in range(1, cols_n)]
    gates = call(
        functools.partial(gates_kernel, cols_n),
        [block, block32] * cols_n,
        pairs + [out_gating],
        flops=100_000_000,
    )
    firsts, lefts = [], []
    for h in range(cols_n):
        mine, other = call(
            outgoing_kernel,
            [shape(half, BF16), shape(half, BF16)],
            [left, core_left] + rights[h * pieces : (h + 1) * pieces],
            scratch=[
                pltpu.VMEM((cols * pieces * rows, chan), F32),
                pltpu.VMEM((rows * cols, chan), F32),
            ],
            flops=500_000_000,
        )
        parts = [mine] + [shift(mine, dx, 0) for dx in range(1, cols_n)]
        parts += [shift(other, dx, 1) for dx in range(cols_n)]
        first, left_mine, left_other = call(
            functools.partial(first_kernel, cols_n, h),
            [block, shape(half, BF16), shape(half, BF16)],
            parts + list(gates[2 * h : 2 * h + 2]) + [mask, out_final, in_project],
            scratch=[
                pltpu.VMEM((rows * cols, chan), F32),
                pltpu.VMEM((rows * pieces * rows, chan), F32),
            ],
            flops=200_000_000,
        )
        firsts.append(first)
        lefts.append([left_mine, along_row(left_other, 1)])

    right, first = call(
        right_kernel, [block, block], firsts + [mask, in_project], flops=100_000_000
    )
    core_right = along_row(right, 1)

    def partial_products(steps):
        used = lefts[steps[0] // pieces : steps[-1] // pieces + 1]
        return call(
            functools.partial(incoming_kernel, steps),
            [block32 if m == 0 else block for m in steps],
            [right, core_right] + sum(used, []),
            scratch=[
                pltpu.VMEM((2 * len(used) * rows * pieces * rows, chan), F32),
                pltpu.VMEM((2 * rows * cols, chan), F32),
            ],
            flops=200_000_000 * len(steps),
        )

    far = list(range(pieces, chips))
    parts = [None] * chips
    for m, value in zip(far, partial_products(far)):
        parts[m] = along_row(value, 2 * m)
    near = list(range(1, pieces))
    for m, value in zip(near, partial_products(near)):
        parts[m] = along_row(value, 2 * m)
    parts[0] = partial_products([0])[0]
    gate = call(gate_kernel, block32, [first, in_gating], flops=50_000_000)
    return call(last_kernel, block, parts + [first, gate, in_final], flops=100_000_000)


def solution(mesh):
    return jax.shard_map(
        functools.partial(on_device, mesh.shape["row"], mesh.shape["col"]),
        mesh=mesh,
        in_specs=(P(("groups", "row"), "col", None), P("groups"), P(), P(), P(), P(), P(), P()),
        out_specs=P(("groups", "row"), "col", None),
        check_vma=False,
    )
```

```python
import functools

import jax
import jax.numpy as jnp
from jax import lax
from jax.experimental import pallas as pl
from jax.experimental.pallas import tpu as pltpu
from jax.sharding import PartitionSpec as P

F32, BF16 = jnp.float32, jnp.bfloat16
VMEM = pl.BlockSpec(memory_space=pltpu.VMEM)
LIMIT = 40 * 1024 * 1024
FULL = 63 * 1024 * 1024


def after(kernel, count, *refs):
    kernel(*refs[count:])


def call(kernel, outs, args, scratch=(), flops=10_000_000, outside=(), limit=LIMIT):
    single = not isinstance(outs, (list, tuple))
    outs = [outs] if single else list(outs)
    moved = sum(a.size * a.dtype.itemsize for a in args) + sum(
        o.size * o.dtype.itemsize for o in outs
    )
    result = pl.pallas_call(
        kernel,
        out_shape=outs,
        in_specs=[
            pl.BlockSpec(memory_space=pl.ANY) if n in outside else VMEM for n in range(len(args))
        ],
        out_specs=[VMEM] * len(outs),
        scratch_shapes=list(scratch),
        compiler_params=pltpu.CompilerParams(vmem_limit_bytes=limit),
        cost_estimate=pl.CostEstimate(flops=flops, bytes_accessed=moved, transcendentals=0),
    )(*args)
    return result[0] if single else result


def shape(dims, dtype):
    return jax.ShapeDtypeStruct(dims, dtype)


def sigmoid(v):
    return 0.5 * jnp.tanh(0.5 * v) + 0.5


def layer_norm(v):
    center = jnp.mean(v, axis=-1, keepdims=True)
    shifted = v - center
    spread = jnp.mean(shifted * shifted, axis=-1, keepdims=True)
    return shifted * lax.rsqrt(spread + 1e-05)


def place():
    row = lax.axis_index("row")
    return row // 2, row % 2, lax.axis_index("col")


def token_weights(mask_row, start, count):
    tokens = mask_row.shape[1]
    lane = lax.broadcasted_iota(jnp.int32, (count, tokens), 1)
    row = lax.broadcasted_iota(jnp.int32, (count, tokens), 0)
    hot = jnp.where(lane == row + start, mask_row, 0.0).astype(BF16)
    return jnp.dot(hot, jnp.ones((tokens, 128), BF16), preferred_element_type=F32)


def gated(normed, w, mask_ref, rows, cols, x):
    hidden = w.shape[1] // 2
    projected = jnp.dot(normed, w, preferred_element_type=F32)
    value = sigmoid(projected[:, hidden:]) * projected[:, :hidden]
    mask_row = mask_ref[...].astype(F32)
    row_w = token_weights(mask_row, lax.axis_index("row") * rows, -(-rows // 8) * 8)
    col_w = token_weights(mask_row, x * cols, cols)
    weights = row_w[:rows, None, :] * col_w[None, :, :]
    return value * weights.reshape(rows * cols, 128)


def normed_of(pair):
    rows, cols, chan = pair.shape
    return layer_norm(pair.astype(F32)).astype(BF16).reshape(rows * cols, chan)


def opening_kernel(pair_hbm, mask_hbm, w_hbm, right_ref, pair_ref, mask_scr, w_scr, sems):
    rows, cols, chan = pair_ref.shape
    width = w_scr.shape[1]
    copies = [
        pltpu.make_async_copy(pair_hbm, pair_ref, sems.at[0]),
        pltpu.make_async_copy(w_hbm.at[:, pl.ds(width, width)], w_scr, sems.at[1]),
        pltpu.make_async_copy(mask_hbm, mask_scr, sems.at[2]),
    ]
    for copy in copies:
        copy.start()
    for copy in copies:
        copy.wait()
    value = gated(
        normed_of(pair_ref[...]), w_scr[...], mask_scr, rows, cols, lax.axis_index("col")
    )
    right_ref[...] = value.astype(BF16).reshape(right_ref.shape)


def left_kernel(pair_ref, mask_ref, w_ref, left_ref, copy_ref):
    rows, cols, _ = pair_ref.shape
    w = w_ref[:, : w_ref.shape[1] // 2]
    value = gated(normed_of(pair_ref[...]), w, mask_ref, rows, cols, lax.axis_index("col"))
    left_ref[...] = value.astype(BF16).reshape(left_ref.shape)
    copy_ref[...] = pair_ref[...]


def gates_kernel(cols_n, *refs):
    pairs, w_ref, outs = refs[:cols_n], refs[cols_n], refs[cols_n + 1 :]
    rows, cols, _ = pairs[0].shape
    pieces = cols // (2 * rows)
    z, _, x = place()
    for h in range(cols_n):
        pair_ref, gate_ref = outs[2 * h : 2 * h + 2]
        for dx in range(cols_n):

            @pl.when(((z // pieces) ^ x ^ h) == dx)
            def _():
                pair_ref[...] = pairs[dx][...]

        gate = jnp.dot(normed_of(pair_ref[...]), w_ref[...], preferred_element_type=F32)
        gate_ref[...] = sigmoid(gate).reshape(gate_ref.shape)


def gate_kernel(pair_ref, w_ref, gate_ref):
    gate = jnp.dot(normed_of(pair_ref[...]), w_ref[...], preferred_element_type=F32)
    gate_ref[...] = sigmoid(gate).reshape(gate_ref.shape)


def outgoing_kernel(runs, own_left, core_left, *refs):
    rights, (mine_ref, other_ref, r_scr, l_scr, o_scr) = refs[:-5], refs[-5:]
    rows, cols, chan = own_left.shape
    z, _, _ = place()
    for out_ref, left in ((mine_ref, own_left), (other_ref, core_left)):
        l_scr[...] = left[...].astype(F32).reshape(rows * cols, chan)
        done = 0
        for count in runs:
            used = count * rows
            width = -(-used // 8) * 8
            if out_ref is mine_ref or len(runs) > 1:
                for m, ref in enumerate(rights[done : done + count]):
                    base = ((z % count) ^ m) * rows
                    for j in range(rows):
                        r_scr[pl.ds(base + j, cols, stride=width), :] = ref[j].astype(F32)

            def step(block, totals):
                for u in range(8):
                    k = block * 8 + u
                    right = r_scr[pl.ds(pl.multiple_of(k * width, 8), width), :]
                    totals = tuple(
                        t + l_scr[pl.ds(i * cols + k, 1), :] * right for i, t in enumerate(totals)
                    )
                return totals

            zero = jnp.zeros((width, chan), F32)
            totals = lax.fori_loop(0, cols // 8, step, (zero,) * rows)
            for i, t in enumerate(totals):
                o_scr[pl.ds(rows * done * rows + i * used, used), :] = t[:used]
            done += count
        out_ref[...] = o_scr[...].astype(BF16)


def first_kernel(cols_n, h, groups, *refs):
    parts, refs = refs[: 2 * cols_n * len(groups)], refs[2 * cols_n * len(groups) :]
    pair_ref, gate_ref, mask_ref, final_ref, w_ref = refs[:5]
    earlier, refs = refs[5:-6], refs[-6:]
    first_ref, right_ref, mine_ref, other_ref, scr, half_scr = refs
    rows, cols, chan = pair_ref.shape
    pieces = cols // (2 * rows)
    z, core, x = place()
    for n, (begin, start, count) in enumerate(groups):
        group = parts[2 * cols_n * n : 2 * cols_n * (n + 1)]
        size = rows * count * rows
        for some, side in ((group[:cols_n], core), (group[cols_n:], 1 - core)):
            value = some[0][pl.ds(begin, size), :].astype(F32)
            for ref in some[1:]:
                value = value + ref[pl.ds(begin, size), :].astype(F32)
            half_scr[pl.ds(0, size), :] = value
            for i in range(rows):
                for p in range(count):
                    q = p if count == pieces else (z % pieces) ^ start
                    part = half_scr[pl.ds((i * count + p) * rows, rows), :]
                    scr[pl.ds(i * cols + (2 * q + side) * rows, rows), :] = part
    mixed = layer_norm(scr[...]).astype(BF16)
    update = jnp.dot(mixed, final_ref[...], preferred_element_type=F32)
    pair = pair_ref[...].astype(F32).reshape(rows * cols, chan)
    first = (pair + gate_ref[...].reshape(rows * cols, chan) * update).astype(BF16)
    first_ref[...] = first.reshape(first_ref.shape)
    normed = layer_norm(first.astype(F32)).astype(BF16)
    width = w_ref.shape[1] // 2
    block = (z // pieces) ^ h
    scr[...] = gated(normed, w_ref[:, :width], mask_ref, rows, cols, block)
    for out_ref, side in ((mine_ref, core), (other_ref, 1 - core)):
        for i in range(rows):
            for q in range(pieces):
                part = scr[pl.ds(i * cols + (2 * q + side) * rows, rows), :]
                half_scr[pl.ds((i * pieces + q) * rows, rows), :] = part
        out_ref[...] = half_scr[...].astype(BF16).reshape(out_ref.shape)
    right = gated(normed, w_ref[:, width:], mask_ref, rows, cols, block)
    right_ref[...] = right.astype(BF16).reshape(right_ref.shape)
    for g in range(len(earlier) // 2):

        @pl.when(((z // pieces) ^ g) == x)
        def _():
            first_ref[...] = earlier[2 * g][...]
            right_ref[...] = earlier[2 * g + 1][...]


def incoming_kernel(steps, *refs):
    own_right, core_right = refs[:2]
    count = (len(refs) - 4 - len(steps)) // 2
    lefts = refs[2 : 2 + 2 * count]
    outs = refs[2 + 2 * count : -2]
    l_scr, r_scr = refs[-2:]
    rows, cols, chan = own_right.shape
    width = lefts[0].shape[1]
    pieces = width // rows
    z, _, _ = place()
    for n, ref in enumerate((own_right, core_right)):
        r_scr[pl.ds(n * rows * cols, rows * cols), :] = ref[...].astype(F32).reshape(-1, chan)
    for n, ref in enumerate(lefts):
        l_scr[pl.ds(n * rows * width, rows * width), :] = ref[...].astype(F32).reshape(-1, chan)
    for m, out_ref in zip(steps, outs):
        block = m // pieces - steps[0] // pieces
        base = block * (2 * rows * width) + ((z ^ m) % pieces) * rows
        for group in range(0, rows, 6):

            def step(k, totals):
                right = r_scr[pl.ds(pl.multiple_of(k * cols, 8), cols), :]
                return tuple(
                    t + l_scr[pl.ds(base + k * width + group + i, 1), :] * right
                    for i, t in enumerate(totals)
                )

            zero = jnp.zeros((cols, chan), F32)
            totals = lax.fori_loop(0, 2 * rows, step, (zero,) * 6, unroll=4)
            for i, t in enumerate(totals):
                out_ref[group + i] = t.astype(out_ref.dtype)


def last_kernel(*refs):
    parts, (first_ref, gate_ref, final_ref, out_ref) = refs[:-4], refs[-4:]
    rows, cols, chan = first_ref.shape
    product = parts[0][...].astype(F32)
    for ref in parts[1:]:
        product = product + ref[...].astype(F32)
    mixed = layer_norm(product).astype(BF16).reshape(rows * cols, chan)
    update = jnp.dot(mixed, final_ref[...], preferred_element_type=F32)
    first = first_ref[...].astype(F32).reshape(rows * cols, chan)
    result = first + gate_ref[...].reshape(rows * cols, chan) * update
    out_ref[...] = result.astype(BF16).reshape(out_ref.shape)


def on_device(
    rows_n,
    cols_n,
    pair_rep,
    token_mask,
    out_project,
    out_gating,
    out_final,
    in_project,
    in_gating,
    in_final,
):
    rows, cols, chan = pair_rep.shape
    chips = rows_n // 2
    pieces = cols // (2 * rows)
    mask = token_mask.reshape(1, -1)
    block = shape((rows, cols, chan), BF16)
    block32 = shape((rows, cols, chan), F32)
    half = (rows, pieces * rows, chan)

    def along_row(v, bits):
        return lax.ppermute(v, "row", [(i, i ^ bits) for i in range(rows_n)])

    def shift(v, dx, core):
        pairs = [
            (r * cols_n + c, (r ^ core) * cols_n + (c ^ dx))
            for r in range(rows_n)
            for c in range(cols_n)
        ]
        return lax.ppermute(v, ("row", "col"), pairs)

    right = call(
        opening_kernel,
        block,
        [pair_rep, mask, out_project],
        scratch=[
            pltpu.VMEM(pair_rep.shape, BF16),
            pltpu.VMEM(mask.shape, jnp.int32),
            pltpu.VMEM((chan, out_project.shape[1] // 2), BF16),
            pltpu.SemaphoreType.DMA((3,)),
        ],
        flops=100_000_000,
        outside=(0, 1, 2),
        limit=FULL,
    )
    rights = {0: right}
    bit = chips // 2
    while bit:
        for m in list(rights):
            rights[m | bit] = along_row(rights[m], 2 * bit)
        bit //= 2
    left, pair_copy = call(
        functools.partial(after, left_kernel, 1),
        [block, block],
        [right, pair_rep, mask, out_project],
        flops=100_000_000,
        outside=(0,),
    )
    pairs = [pair_copy] + [shift(pair_copy, dx, 0) for dx in range(1, cols_n)]
    gates = call(
        functools.partial(gates_kernel, cols_n),
        [block, block32] * cols_n,
        pairs + [out_gating],
        flops=100_000_000,
    )
    core_left = along_row(left, 1)
    runs = [pieces] * (cols_n - 1) + [1] * (pieces - 1)
    exchanged = []
    for counts, blocks in ((runs, list(range(chips - 1))), ([1], [chips - 1])):
        out = shape((rows * len(blocks) * rows, chan), BF16)
        mine, other = call(
            functools.partial(outgoing_kernel, counts),
            [out, out],
            [left, core_left] + [rights[m] for m in blocks],
            scratch=[
                pltpu.VMEM((cols * (-(-max(counts) * rows // 8) * 8), chan), F32),
                pltpu.VMEM((rows * cols, chan), F32),
                pltpu.VMEM(out.shape, F32),
            ],
            flops=250_000_000 * len(blocks),
        )
        parts = [mine] + [shift(mine, dx, 0) for dx in range(1, cols_n)]
        exchanged.append(parts + [shift(other, dx, 1) for dx in range(cols_n)])
    firsts, lefts = [], []
    for h in range(cols_n):
        area = rows * rows
        if h < cols_n - 1:
            groups, parts, earlier = [(h * pieces * area, 0, pieces)], exchanged[0], []
        else:
            groups = [((h * pieces + p) * area, p, 1) for p in range(pieces - 1)]
            groups.append((0, pieces - 1, 1))
            parts, earlier = exchanged[0] * (pieces - 1) + exchanged[1], firsts
        first, right, left_mine, left_other = call(
            functools.partial(first_kernel, cols_n, h, groups),
            [block, block, shape(half, BF16), shape(half, BF16)],
            parts + list(gates[2 * h : 2 * h + 2]) + [mask, out_final, in_project] + earlier,
            scratch=[
                pltpu.VMEM((rows * cols, chan), F32),
                pltpu.VMEM((rows * pieces * rows, chan), F32),
            ],
            flops=300_000_000,
        )
        firsts += [first, right]
        lefts.append([left_mine, along_row(left_other, 1)])

    core_right = along_row(right, 1)

    def partial_products(steps):
        used = lefts[steps[0] // pieces : steps[-1] // pieces + 1]
        return call(
            functools.partial(incoming_kernel, steps),
            [block if m else block32 for m in steps],
            [right, core_right] + sum(used, []),
            scratch=[
                pltpu.VMEM((2 * len(used) * rows * pieces * rows, chan), F32),
                pltpu.VMEM((2 * rows * cols, chan), F32),
            ],
            flops=200_000_000 * len(steps),
        )

    parts = [None] * chips
    far, near = list(range(pieces, chips)), list(range(1, pieces))
    for m, value in zip(far, partial_products(far)):
        parts[m] = along_row(value, 2 * m)
    for m, value in zip(near, partial_products(near)):
        parts[m] = along_row(value, 2 * m)
    parts[0] = partial_products([0])[0]
    gate = call(gate_kernel, block32, [first, in_gating], flops=50_000_000)
    return call(last_kernel, block, parts + [first, gate, in_final], flops=100_000_000)


def solution(mesh):
    return jax.shard_map(
        functools.partial(on_device, mesh.shape["row"], mesh.shape["col"]),
        mesh=mesh,
        in_specs=(P(("groups", "row"), "col", None), P("groups"), P(), P(), P(), P(), P(), P()),
        out_specs=P(("groups", "row"), "col", None),
        check_vma=False,
    )
```

```python
import functools

import jax
import jax.numpy as jnp
from jax import lax
from jax.experimental import pallas as pl
from jax.experimental.pallas import tpu as pltpu
from jax.sharding import PartitionSpec as P

F32, BF16 = jnp.float32, jnp.bfloat16
VMEM = pl.BlockSpec(memory_space=pltpu.VMEM)
LIMIT = 40 * 1024 * 1024
FULL = 63 * 1024 * 1024


def after(kernel, count, *refs):
    kernel(*refs[count:])


def call(kernel, outs, args, scratch=(), flops=10_000_000, outside=(), limit=LIMIT):
    single = not isinstance(outs, (list, tuple))
    outs = [outs] if single else list(outs)
    moved = sum(a.size * a.dtype.itemsize for a in args) + sum(
        o.size * o.dtype.itemsize for o in outs
    )
    result = pl.pallas_call(
        kernel,
        out_shape=outs,
        in_specs=[
            pl.BlockSpec(memory_space=pl.ANY) if n in outside else VMEM for n in range(len(args))
        ],
        out_specs=[VMEM] * len(outs),
        scratch_shapes=list(scratch),
        compiler_params=pltpu.CompilerParams(vmem_limit_bytes=limit),
        cost_estimate=pl.CostEstimate(flops=flops, bytes_accessed=moved, transcendentals=0),
    )(*args)
    return result[0] if single else result


def shape(dims, dtype):
    return jax.ShapeDtypeStruct(dims, dtype)


def sigmoid(v):
    return 0.5 * jnp.tanh(0.5 * v) + 0.5


def layer_norm(v):
    center = jnp.mean(v, axis=-1, keepdims=True)
    shifted = v - center
    spread = jnp.mean(shifted * shifted, axis=-1, keepdims=True)
    return shifted * lax.rsqrt(spread + 1e-05)


def place():
    row = lax.axis_index("row")
    return row // 2, row % 2, lax.axis_index("col")


def token_weights(mask_row, start, count):
    tokens = mask_row.shape[1]
    lane = lax.broadcasted_iota(jnp.int32, (count, tokens), 1)
    row = lax.broadcasted_iota(jnp.int32, (count, tokens), 0)
    hot = jnp.where(lane == row + start, mask_row, 0.0).astype(BF16)
    return jnp.dot(hot, jnp.ones((tokens, 128), BF16), preferred_element_type=F32)


def gated(normed, w, mask_ref, rows, cols, x):
    hidden = w.shape[1] // 2
    projected = jnp.dot(normed, w, preferred_element_type=F32)
    value = sigmoid(projected[:, hidden:]) * projected[:, :hidden]
    mask_row = mask_ref[...].astype(F32)
    row_w = token_weights(mask_row, lax.axis_index("row") * rows, -(-rows // 8) * 8)
    col_w = token_weights(mask_row, x * cols, cols)
    weights = row_w[:rows, None, :] * col_w[None, :, :]
    return value * weights.reshape(rows * cols, 128)


def normed_of(pair):
    rows, cols, chan = pair.shape
    return layer_norm(pair.astype(F32)).astype(BF16).reshape(rows * cols, chan)


def opening_kernel(pair_hbm, mask_hbm, w_hbm, right_ref, pair_ref, mask_scr, w_scr, sems):
    rows, cols, chan = pair_ref.shape
    width = w_scr.shape[1]
    copies = [
        pltpu.make_async_copy(pair_hbm, pair_ref, sems.at[0]),
        pltpu.make_async_copy(w_hbm.at[:, pl.ds(width, width)], w_scr, sems.at[1]),
        pltpu.make_async_copy(mask_hbm, mask_scr, sems.at[2]),
    ]
    for copy in copies:
        copy.start()
    for copy in copies:
        copy.wait()
    value = gated(
        normed_of(pair_ref[...]), w_scr[...], mask_scr, rows, cols, lax.axis_index("col")
    )
    right_ref[...] = value.astype(BF16).reshape(right_ref.shape)


def left_kernel(pair_ref, mask_ref, w_ref, left_ref, copy_ref):
    rows, cols, _ = pair_ref.shape
    w = w_ref[:, : w_ref.shape[1] // 2]
    value = gated(normed_of(pair_ref[...]), w, mask_ref, rows, cols, lax.axis_index("col"))
    left_ref[...] = value.astype(BF16).reshape(left_ref.shape)
    copy_ref[...] = pair_ref[...]


def gates_kernel(cols_n, *refs):
    pairs, w_ref, outs = refs[:cols_n], refs[cols_n], refs[cols_n + 1 :]
    rows, cols, _ = pairs[0].shape
    pieces = cols // (2 * rows)
    z, _, x = place()
    for h in range(cols_n):
        pair_ref, gate_ref = outs[2 * h : 2 * h + 2]
        for dx in range(cols_n):

            @pl.when(((z // pieces) ^ x ^ h) == dx)
            def _():
                pair_ref[...] = pairs[dx][...]

        gate = jnp.dot(normed_of(pair_ref[...]), w_ref[...], preferred_element_type=F32)
        gate_ref[...] = sigmoid(gate).reshape(gate_ref.shape)


def gate_kernel(pair_ref, w_ref, gate_ref):
    gate = jnp.dot(normed_of(pair_ref[...]), w_ref[...], preferred_element_type=F32)
    gate_ref[...] = sigmoid(gate).reshape(gate_ref.shape)


def outgoing_kernel(carried, *refs):
    earlier, (own_left, core_left), refs = refs[:carried], refs[carried : carried + 2], refs[carried + 2 :]
    rights, (mine_ref, other_ref, r_scr, l_scr, o_scr) = refs[:-5], refs[-5:]
    rows, cols, chan = own_left.shape
    count = len(rights)
    used = count * rows
    width = -(-used // 8) * 8
    z, _, _ = place()
    begin = earlier[0].shape[0] if carried else 0
    for m, ref in enumerate(rights):
        base = ((z % count) ^ m) * rows
        for j in range(rows):
            r_scr[pl.ds(base + j, cols, stride=width), :] = ref[j].astype(F32)
    for n, (out_ref, left) in enumerate(((mine_ref, own_left), (other_ref, core_left))):
        l_scr[...] = left[...].astype(F32).reshape(rows * cols, chan)

        def step(block, totals):
            for u in range(8):
                k = block * 8 + u
                right = r_scr[pl.ds(pl.multiple_of(k * width, 8), width), :]
                totals = tuple(
                    t + l_scr[pl.ds(i * cols + k, 1), :] * right for i, t in enumerate(totals)
                )
            return totals

        zero = jnp.zeros((width, chan), F32)
        totals = lax.fori_loop(0, cols // 8, step, (zero,) * rows)
        for i, t in enumerate(totals):
            o_scr[pl.ds(i * used, used), :] = t[:used]
        if carried:
            out_ref[pl.ds(0, begin), :] = earlier[n][...]
        out_ref[pl.ds(begin, rows * used), :] = o_scr[...].astype(BF16)


def first_kernel(cols_n, h, groups, *refs):
    parts, refs = refs[: 2 * cols_n * len(groups)], refs[2 * cols_n * len(groups) :]
    pair_ref, gate_ref, mask_ref, final_ref, w_ref = refs[:5]
    earlier, refs = refs[5:-6], refs[-6:]
    first_ref, right_ref, mine_ref, other_ref, scr, half_scr = refs
    rows, cols, chan = pair_ref.shape
    pieces = cols // (2 * rows)
    z, core, x = place()
    for n, (begin, start, count) in enumerate(groups):
        group = parts[2 * cols_n * n : 2 * cols_n * (n + 1)]
        size = rows * count * rows
        for some, side in ((group[:cols_n], core), (group[cols_n:], 1 - core)):
            value = some[0][pl.ds(begin, size), :].astype(F32)
            for ref in some[1:]:
                value = value + ref[pl.ds(begin, size), :].astype(F32)
            half_scr[pl.ds(0, size), :] = value
            for i in range(rows):
                for p in range(count):
                    q = p if count == pieces else (z % pieces) ^ start
                    part = half_scr[pl.ds((i * count + p) * rows, rows), :]
                    scr[pl.ds(i * cols + (2 * q + side) * rows, rows), :] = part
    mixed = layer_norm(scr[...]).astype(BF16)
    update = jnp.dot(mixed, final_ref[...], preferred_element_type=F32)
    pair = pair_ref[...].astype(F32).reshape(rows * cols, chan)
    first = (pair + gate_ref[...].reshape(rows * cols, chan) * update).astype(BF16)
    first_ref[...] = first.reshape(first_ref.shape)
    normed = layer_norm(first.astype(F32)).astype(BF16)
    width = w_ref.shape[1] // 2
    block = (z // pieces) ^ h
    scr[...] = gated(normed, w_ref[:, :width], mask_ref, rows, cols, block)
    for out_ref, side in ((mine_ref, core), (other_ref, 1 - core)):
        for i in range(rows):
            for q in range(pieces):
                part = scr[pl.ds(i * cols + (2 * q + side) * rows, rows), :]
                half_scr[pl.ds((i * pieces + q) * rows, rows), :] = part
        out_ref[...] = half_scr[...].astype(BF16).reshape(out_ref.shape)
    right = gated(normed, w_ref[:, width:], mask_ref, rows, cols, block)
    right_ref[...] = right.astype(BF16).reshape(right_ref.shape)
    for g in range(len(earlier) // 2):

        @pl.when(((z // pieces) ^ g) == x)
        def _():
            first_ref[...] = earlier[2 * g][...]
            right_ref[...] = earlier[2 * g + 1][...]


def incoming_kernel(steps, *refs):
    own_right, core_right = refs[:2]
    count = (len(refs) - 4 - len(steps)) // 2
    lefts = refs[2 : 2 + 2 * count]
    outs = refs[2 + 2 * count : -2]
    l_scr, r_scr = refs[-2:]
    rows, cols, chan = own_right.shape
    width = lefts[0].shape[1]
    pieces = width // rows
    z, _, _ = place()
    for n, ref in enumerate((own_right, core_right)):
        r_scr[pl.ds(n * rows * cols, rows * cols), :] = ref[...].astype(F32).reshape(-1, chan)
    for n, ref in enumerate(lefts):
        l_scr[pl.ds(n * rows * width, rows * width), :] = ref[...].astype(F32).reshape(-1, chan)
    for m, out_ref in zip(steps, outs):
        block = m // pieces - steps[0] // pieces
        base = block * (2 * rows * width) + ((z ^ m) % pieces) * rows
        for group in range(0, rows, 6):

            def step(k, totals):
                right = r_scr[pl.ds(pl.multiple_of(k * cols, 8), cols), :]
                return tuple(
                    t + l_scr[pl.ds(base + k * width + group + i, 1), :] * right
                    for i, t in enumerate(totals)
                )

            zero = jnp.zeros((cols, chan), F32)
            totals = lax.fori_loop(0, 2 * rows, step, (zero,) * 6, unroll=4)
            for i, t in enumerate(totals):
                out_ref[group + i] = t.astype(out_ref.dtype)


def last_kernel(*refs):
    parts, (first_ref, gate_ref, final_ref, out_ref) = refs[:-4], refs[-4:]
    rows, cols, chan = first_ref.shape
    product = parts[0][...].astype(F32)
    for ref in parts[1:]:
        product = product + ref[...].astype(F32)
    mixed = layer_norm(product).astype(BF16).reshape(rows * cols, chan)
    update = jnp.dot(mixed, final_ref[...], preferred_element_type=F32)
    first = first_ref[...].astype(F32).reshape(rows * cols, chan)
    result = first + gate_ref[...].reshape(rows * cols, chan) * update
    out_ref[...] = result.astype(BF16).reshape(out_ref.shape)


def on_device(
    rows_n,
    cols_n,
    pair_rep,
    token_mask,
    out_project,
    out_gating,
    out_final,
    in_project,
    in_gating,
    in_final,
):
    rows, cols, chan = pair_rep.shape
    chips = rows_n // 2
    pieces = cols // (2 * rows)
    mask = token_mask.reshape(1, -1)
    block = shape((rows, cols, chan), BF16)
    block32 = shape((rows, cols, chan), F32)
    half = (rows, pieces * rows, chan)

    def along_row(v, bits):
        return lax.ppermute(v, "row", [(i, i ^ bits) for i in range(rows_n)])

    def shift(v, dx, core):
        pairs = [
            (r * cols_n + c, (r ^ core) * cols_n + (c ^ dx))
            for r in range(rows_n)
            for c in range(cols_n)
        ]
        return lax.ppermute(v, ("row", "col"), pairs)

    right = call(
        opening_kernel,
        block,
        [pair_rep, mask, out_project],
        scratch=[
            pltpu.VMEM(pair_rep.shape, BF16),
            pltpu.VMEM(mask.shape, jnp.int32),
            pltpu.VMEM((chan, out_project.shape[1] // 2), BF16),
            pltpu.SemaphoreType.DMA((3,)),
        ],
        flops=100_000_000,
        outside=(0, 1, 2),
        limit=FULL,
    )
    rights = {0: right}
    bit = chips // 2
    while bit:
        for m in list(rights):
            rights[m | bit] = along_row(rights[m], 2 * bit)
        bit //= 2
    left, pair_copy = call(
        functools.partial(after, left_kernel, 1),
        [block, block],
        [right, pair_rep, mask, out_project],
        flops=100_000_000,
        outside=(0,),
    )
    pairs = [pair_copy] + [shift(pair_copy, dx, 0) for dx in range(1, cols_n)]
    gates = call(
        functools.partial(gates_kernel, cols_n),
        [block, block32] * cols_n,
        pairs + [out_gating],
        flops=100_000_000,
    )
    core_left = along_row(left, 1)
    def product(blocks, earlier, wait=()):
        size = rows * len(blocks) * rows
        out = shape((size + sum(e.shape[0] for e in earlier[:1]), chan), BF16)
        return call(
            functools.partial(
                after, functools.partial(outgoing_kernel, len(earlier)), len(wait)
            ),
            [out, out],
            [*wait, *earlier, left, core_left] + [rights[m] for m in blocks],
            scratch=[
                pltpu.VMEM((cols * (-(-len(blocks) * rows // 8) * 8), chan), F32),
                pltpu.VMEM((rows * cols, chan), F32),
                pltpu.VMEM((size, chan), F32),
            ],
            flops=250_000_000 * len(blocks),
            outside=range(len(wait)),
        )

    early = []
    for h in range(cols_n - 1):
        early = product(range(h * pieces, (h + 1) * pieces), early)
    for m in range(chips - pieces, chips - 1):
        early = product([m], early)
    exchanged = []
    for mine, other in (early, product([chips - 1], [], gates[1:2])):
        parts = [mine] + [shift(mine, dx, 0) for dx in range(1, cols_n)]
        exchanged.append(parts + [shift(other, dx, 1) for dx in range(cols_n)])
    firsts, lefts = [], []
    for h in range(cols_n):
        area = rows * rows
        if h < cols_n - 1:
            groups, parts, earlier = [(h * pieces * area, 0, pieces)], exchanged[0], []
        else:
            groups = [((h * pieces + p) * area, p, 1) for p in range(pieces - 1)]
            groups.append((0, pieces - 1, 1))
            parts, earlier = exchanged[0] * (pieces - 1) + exchanged[1], firsts
        first, right, left_mine, left_other = call(
            functools.partial(first_kernel, cols_n, h, groups),
            [block, block, shape(half, BF16), shape(half, BF16)],
            parts + list(gates[2 * h : 2 * h + 2]) + [mask, out_final, in_project] + earlier,
            scratch=[
                pltpu.VMEM((rows * cols, chan), F32),
                pltpu.VMEM((rows * pieces * rows, chan), F32),
            ],
            flops=300_000_000,
        )
        firsts += [first, right]
        lefts.append([left_mine, along_row(left_other, 1)])

    core_right = along_row(right, 1)

    def partial_products(steps):
        used = lefts[steps[0] // pieces : steps[-1] // pieces + 1]
        wait = [] if used[-1] is lefts[-1] else lefts[-1]
        return call(
            functools.partial(after, functools.partial(incoming_kernel, steps), len(wait)),
            [block if m else block32 for m in steps],
            wait + [right, core_right] + sum(used, []),
            scratch=[
                pltpu.VMEM((2 * len(used) * rows * pieces * rows, chan), F32),
                pltpu.VMEM((2 * rows * cols, chan), F32),
            ],
            flops=200_000_000 * len(steps),
            outside=range(len(wait)),
        )

    parts = [None] * chips
    for m, value in enumerate(partial_products(list(range(pieces, chips))), pieces):
        parts[m] = along_row(value, 2 * m)
    for m in reversed(range(pieces)):
        value = partial_products([m])[0]
        parts[m] = along_row(value, 2 * m) if m else value
    gate = call(gate_kernel, block32, [first, in_gating], flops=50_000_000)
    return call(last_kernel, block, parts + [first, gate, in_final], flops=100_000_000)


def solution(mesh):
    return jax.shard_map(
        functools.partial(on_device, mesh.shape["row"], mesh.shape["col"]),
        mesh=mesh,
        in_specs=(P(("groups", "row"), "col", None), P("groups"), P(), P(), P(), P(), P(), P()),
        out_specs=P(("groups", "row"), "col", None),
        check_vma=False,
    )
```

```python
import functools

import jax
import jax.numpy as jnp
from jax import lax
from jax.experimental import pallas as pl
from jax.experimental.pallas import tpu as pltpu
from jax.sharding import PartitionSpec as P

F32, BF16 = jnp.float32, jnp.bfloat16
VMEM = pl.BlockSpec(memory_space=pltpu.VMEM)
LIMIT = 40 * 1024 * 1024
FULL = 63 * 1024 * 1024


def after(kernel, count, *refs):
    kernel(*refs[count:])


def call(kernel, outs, args, scratch=(), flops=10_000_000, outside=(), limit=LIMIT):
    single = not isinstance(outs, (list, tuple))
    outs = [outs] if single else list(outs)
    moved = sum(a.size * a.dtype.itemsize for a in args) + sum(
        o.size * o.dtype.itemsize for o in outs
    )
    result = pl.pallas_call(
        kernel,
        out_shape=outs,
        in_specs=[
            pl.BlockSpec(memory_space=pl.ANY) if n in outside else VMEM for n in range(len(args))
        ],
        out_specs=[VMEM] * len(outs),
        scratch_shapes=list(scratch),
        compiler_params=pltpu.CompilerParams(vmem_limit_bytes=limit),
        cost_estimate=pl.CostEstimate(flops=flops, bytes_accessed=moved, transcendentals=0),
    )(*args)
    return result[0] if single else result


def shape(dims, dtype):
    return jax.ShapeDtypeStruct(dims, dtype)


def sigmoid(v):
    return 0.5 * jnp.tanh(0.5 * v) + 0.5


def layer_norm(v):
    center = jnp.mean(v, axis=-1, keepdims=True)
    shifted = v - center
    spread = jnp.mean(shifted * shifted, axis=-1, keepdims=True)
    return shifted * lax.rsqrt(spread + 1e-05)


def place():
    row = lax.axis_index("row")
    return row // 2, row % 2, lax.axis_index("col")


def token_weights(mask_row, start, count):
    tokens = mask_row.shape[1]
    lane = lax.broadcasted_iota(jnp.int32, (count, tokens), 1)
    row = lax.broadcasted_iota(jnp.int32, (count, tokens), 0)
    hot = jnp.where(lane == row + start, mask_row, 0.0).astype(BF16)
    return jnp.dot(hot, jnp.ones((tokens, 128), BF16), preferred_element_type=F32)


def gated(normed, w, mask_ref, rows, cols, x):
    hidden = w.shape[1] // 2
    projected = jnp.dot(normed, w, preferred_element_type=F32)
    value = sigmoid(projected[:, hidden:]) * projected[:, :hidden]
    mask_row = mask_ref[...].astype(F32)
    row_w = token_weights(mask_row, lax.axis_index("row") * rows, -(-rows // 8) * 8)
    col_w = token_weights(mask_row, x * cols, cols)
    weights = row_w[:rows, None, :] * col_w[None, :, :]
    return value * weights.reshape(rows * cols, 128)


def normed_of(pair):
    rows, cols, chan = pair.shape
    return layer_norm(pair.astype(F32)).astype(BF16).reshape(rows * cols, chan)


def opening_kernel(pair_hbm, mask_hbm, w_hbm, right_ref, pair_ref, mask_scr, w_scr, sems):
    rows, cols, chan = pair_ref.shape
    width = w_scr.shape[1]
    copies = [
        pltpu.make_async_copy(pair_hbm, pair_ref, sems.at[0]),
        pltpu.make_async_copy(w_hbm.at[:, pl.ds(width, width)], w_scr, sems.at[1]),
        pltpu.make_async_copy(mask_hbm, mask_scr, sems.at[2]),
    ]
    for copy in copies:
        copy.start()
    for copy in copies:
        copy.wait()
    value = gated(
        normed_of(pair_ref[...]), w_scr[...], mask_scr, rows, cols, lax.axis_index("col")
    )
    right_ref[...] = value.astype(BF16).reshape(right_ref.shape)


def left_kernel(pair_ref, mask_ref, w_ref, left_ref, copy_ref):
    rows, cols, _ = pair_ref.shape
    w = w_ref[:, : w_ref.shape[1] // 2]
    value = gated(normed_of(pair_ref[...]), w, mask_ref, rows, cols, lax.axis_index("col"))
    left_ref[...] = value.astype(BF16).reshape(left_ref.shape)
    copy_ref[...] = pair_ref[...]


def gates_kernel(cols_n, *refs):
    pairs, w_ref, outs = refs[:cols_n], refs[cols_n], refs[cols_n + 1 :]
    rows, cols, _ = pairs[0].shape
    pieces = cols // (2 * rows)
    z, _, x = place()
    for h in range(cols_n):
        pair_ref, gate_ref = outs[2 * h : 2 * h + 2]
        for dx in range(cols_n):

            @pl.when(((z // pieces) ^ x ^ h) == dx)
            def _():
                pair_ref[...] = pairs[dx][...]

        gate = jnp.dot(normed_of(pair_ref[...]), w_ref[...], preferred_element_type=F32)
        gate_ref[...] = sigmoid(gate).reshape(gate_ref.shape)


def gate_kernel(pair_ref, w_ref, gate_ref):
    gate = jnp.dot(normed_of(pair_ref[...]), w_ref[...], preferred_element_type=F32)
    gate_ref[...] = sigmoid(gate).reshape(gate_ref.shape)


def outgoing_kernel(carried, sides, *refs):
    earlier, lefts, refs = refs[:carried], refs[carried : carried + sides], refs[carried + sides :]
    rights, outs, (r_scr, l_scr, o_scr) = refs[: -3 - sides], refs[-3 - sides : -3], refs[-3:]
    rows, cols, chan = lefts[0].shape
    blocks = len(rights)
    used = blocks * rows
    width = -(-used // 8) * 8
    z, _, _ = place()
    for m, ref in enumerate(rights):
        base = ((z % blocks) ^ m) * rows
        for j in range(rows):
            r_scr[pl.ds(base + j, cols, stride=width), :] = ref[j].astype(F32)
    for n, (left, out_ref) in enumerate(zip(lefts, outs)):
        l_scr[...] = left[...].astype(F32).reshape(rows * cols, chan)

        def step(block, totals):
            for u in range(8):
                k = block * 8 + u
                right = r_scr[pl.ds(pl.multiple_of(k * width, 8), width), :]
                totals = tuple(
                    t + l_scr[pl.ds(i * cols + k, 1), :] * right for i, t in enumerate(totals)
                )
            return totals

        zero = jnp.zeros((width, chan), F32)
        totals = lax.fori_loop(0, cols // 8, step, (zero,) * rows)
        for i, t in enumerate(totals):
            o_scr[pl.ds(i * used, used), :] = t[:used]
        begin = out_ref.shape[0] - rows * used
        if carried:
            out_ref[pl.ds(0, begin), :] = earlier[n][...]
        out_ref[pl.ds(begin, rows * used), :] = o_scr[...].astype(BF16)


def first_kernel(cols_n, h, groups, *refs):
    parts, refs = refs[: 2 * cols_n * len(groups)], refs[2 * cols_n * len(groups) :]
    pair_ref, gate_ref, mask_ref, final_ref, w_ref = refs[:5]
    earlier, refs = refs[5:-6], refs[-6:]
    first_ref, right_ref, mine_ref, other_ref, scr, half_scr = refs
    rows, cols, chan = pair_ref.shape
    pieces = cols // (2 * rows)
    z, core, x = place()
    for n, (begin, start, count) in enumerate(groups):
        group = parts[2 * cols_n * n : 2 * cols_n * (n + 1)]
        size = rows * count * rows
        for some, side in ((group[:cols_n], core), (group[cols_n:], 1 - core)):
            value = some[0][pl.ds(begin, size), :].astype(F32)
            for ref in some[1:]:
                value = value + ref[pl.ds(begin, size), :].astype(F32)
            half_scr[pl.ds(0, size), :] = value
            for i in range(rows):
                for p in range(count):
                    q = p if count == pieces else (z % pieces) ^ start
                    part = half_scr[pl.ds((i * count + p) * rows, rows), :]
                    scr[pl.ds(i * cols + (2 * q + side) * rows, rows), :] = part
    mixed = layer_norm(scr[...]).astype(BF16)
    update = jnp.dot(mixed, final_ref[...], preferred_element_type=F32)
    pair = pair_ref[...].astype(F32).reshape(rows * cols, chan)
    first = (pair + gate_ref[...].reshape(rows * cols, chan) * update).astype(BF16)
    first_ref[...] = first.reshape(first_ref.shape)
    normed = layer_norm(first.astype(F32)).astype(BF16)
    width = w_ref.shape[1] // 2
    block = (z // pieces) ^ h
    scr[...] = gated(normed, w_ref[:, :width], mask_ref, rows, cols, block)
    for out_ref, side in ((mine_ref, core), (other_ref, 1 - core)):
        for i in range(rows):
            for q in range(pieces):
                part = scr[pl.ds(i * cols + (2 * q + side) * rows, rows), :]
                half_scr[pl.ds((i * pieces + q) * rows, rows), :] = part
        out_ref[...] = half_scr[...].astype(BF16).reshape(out_ref.shape)
    right = gated(normed, w_ref[:, width:], mask_ref, rows, cols, block)
    right_ref[...] = right.astype(BF16).reshape(right_ref.shape)
    for g in range(len(earlier) // 2):

        @pl.when(((z // pieces) ^ g) == x)
        def _():
            first_ref[...] = earlier[2 * g][...]
            right_ref[...] = earlier[2 * g + 1][...]


def incoming_kernel(steps, *refs):
    own_right, core_right = refs[:2]
    count = (len(refs) - 4 - len(steps)) // 2
    lefts = refs[2 : 2 + 2 * count]
    outs = refs[2 + 2 * count : -2]
    l_scr, r_scr = refs[-2:]
    rows, cols, chan = own_right.shape
    width = lefts[0].shape[1]
    pieces = width // rows
    z, _, _ = place()
    for n, ref in enumerate((own_right, core_right)):
        r_scr[pl.ds(n * rows * cols, rows * cols), :] = ref[...].astype(F32).reshape(-1, chan)
    for n, ref in enumerate(lefts):
        l_scr[pl.ds(n * rows * width, rows * width), :] = ref[...].astype(F32).reshape(-1, chan)
    for m, out_ref in zip(steps, outs):
        block = m // pieces - steps[0] // pieces
        base = block * (2 * rows * width) + ((z ^ m) % pieces) * rows
        for group in range(0, rows, 6):

            def step(k, totals):
                right = r_scr[pl.ds(pl.multiple_of(k * cols, 8), cols), :]
                return tuple(
                    t + l_scr[pl.ds(base + k * width + group + i, 1), :] * right
                    for i, t in enumerate(totals)
                )

            zero = jnp.zeros((cols, chan), F32)
            totals = lax.fori_loop(0, 2 * rows, step, (zero,) * 6, unroll=4)
            for i, t in enumerate(totals):
                out_ref[group + i] = t.astype(out_ref.dtype)


def last_kernel(*refs):
    parts, (first_ref, gate_ref, final_ref, out_ref) = refs[:-4], refs[-4:]
    rows, cols, chan = first_ref.shape
    product = parts[0][...].astype(F32)
    for ref in parts[1:]:
        product = product + ref[...].astype(F32)
    mixed = layer_norm(product).astype(BF16).reshape(rows * cols, chan)
    update = jnp.dot(mixed, final_ref[...], preferred_element_type=F32)
    first = first_ref[...].astype(F32).reshape(rows * cols, chan)
    result = first + gate_ref[...].reshape(rows * cols, chan) * update
    out_ref[...] = result.astype(BF16).reshape(out_ref.shape)


def on_device(
    rows_n,
    cols_n,
    pair_rep,
    token_mask,
    out_project,
    out_gating,
    out_final,
    in_project,
    in_gating,
    in_final,
):
    rows, cols, chan = pair_rep.shape
    chips = rows_n // 2
    pieces = cols // (2 * rows)
    mask = token_mask.reshape(1, -1)
    block = shape((rows, cols, chan), BF16)
    block32 = shape((rows, cols, chan), F32)
    half = (rows, pieces * rows, chan)

    def along_row(v, bits):
        return lax.ppermute(v, "row", [(i, i ^ bits) for i in range(rows_n)])

    def shift(v, dx, core):
        pairs = [
            (r * cols_n + c, (r ^ core) * cols_n + (c ^ dx))
            for r in range(rows_n)
            for c in range(cols_n)
        ]
        return lax.ppermute(v, ("row", "col"), pairs)

    right = call(
        opening_kernel,
        block,
        [pair_rep, mask, out_project],
        scratch=[
            pltpu.VMEM(pair_rep.shape, BF16),
            pltpu.VMEM(mask.shape, jnp.int32),
            pltpu.VMEM((chan, out_project.shape[1] // 2), BF16),
            pltpu.SemaphoreType.DMA((3,)),
        ],
        flops=100_000_000,
        outside=(0, 1, 2),
        limit=FULL,
    )
    rights = {0: right}
    bit = chips // 2
    while bit:
        for m in list(rights):
            rights[m | bit] = along_row(rights[m], 2 * bit)
        bit //= 2
    left, pair_copy = call(
        functools.partial(after, left_kernel, 1),
        [block, block],
        [right, pair_rep, mask, out_project],
        flops=100_000_000,
        outside=(0,),
    )
    pairs = [pair_copy] + [shift(pair_copy, dx, 0) for dx in range(1, cols_n)]
    gates = call(
        functools.partial(gates_kernel, cols_n),
        [block, block32] * cols_n,
        pairs + [out_gating],
        flops=100_000_000,
    )
    gates = list(gates)
    core_left = along_row(left, 1)
    def product(blocks, sides, earlier=()):
        area = rows * len(blocks) * rows
        out = shape((area + sum(e.shape[0] for e in earlier[:1]), chan), BF16)
        return call(
            functools.partial(outgoing_kernel, len(earlier), len(sides)),
            [out] * len(sides),
            [*earlier, *sides] + [rights[m] for m in blocks],
            scratch=[
                pltpu.VMEM((cols * (-(-len(blocks) * rows // 8) * 8), chan), F32),
                pltpu.VMEM((rows * cols, chan), F32),
                pltpu.VMEM((area, chan), F32),
            ],
            flops=125_000_000 * len(blocks) * len(sides),
        )

    both = [left, core_left]
    early = []
    for h in range(cols_n - 1):
        early = product(range(h * pieces, (h + 1) * pieces), both, early)
    for m in range(chips - pieces, chips - 1):
        early = product([m], both, early)
    mine, other = early
    parts = [mine] + [shift(mine, dx, 0) for dx in range(1, cols_n)]
    exchanged = [parts + [shift(other, dx, 1) for dx in range(cols_n)]]
    (mine,) = product([chips - 1], [left])
    mine, core_left = lax.optimization_barrier((mine, core_left))
    (other,) = product([chips - 1], [core_left])
    other_core, gates[1] = lax.optimization_barrier((other, gates[1]))
    parts = [mine] + [shift(mine, dx, 0) for dx in range(1, cols_n)]
    parts += [shift(other_core, 0, 1)] + [shift(other, dx, 1) for dx in range(1, cols_n)]
    exchanged.append(parts)
    firsts, lefts = [], []
    for h in range(cols_n):
        area = rows * rows
        if h < cols_n - 1:
            groups, parts, earlier = [(h * pieces * area, 0, pieces)], exchanged[0], []
        else:
            groups = [((h * pieces + p) * area, p, 1) for p in range(pieces - 1)]
            groups.append((0, pieces - 1, 1))
            parts, earlier = exchanged[0] * (pieces - 1) + exchanged[1], firsts
        first, right, left_mine, left_other = call(
            functools.partial(first_kernel, cols_n, h, groups),
            [block, block, shape(half, BF16), shape(half, BF16)],
            parts + list(gates[2 * h : 2 * h + 2]) + [mask, out_final, in_project] + earlier,
            scratch=[
                pltpu.VMEM((rows * cols, chan), F32),
                pltpu.VMEM((rows * pieces * rows, chan), F32),
            ],
            flops=300_000_000,
        )
        firsts += [first, right]
        lefts.append([left_mine, along_row(left_other, 1)])

    core_right = along_row(right, 1)

    def partial_products(steps):
        used = lefts[steps[0] // pieces : steps[-1] // pieces + 1]
        wait = [] if used[-1] is lefts[-1] else lefts[-1]
        return call(
            functools.partial(after, functools.partial(incoming_kernel, steps), len(wait)),
            [block if m else block32 for m in steps],
            wait + [right, core_right] + sum(used, []),
            scratch=[
                pltpu.VMEM((2 * len(used) * rows * pieces * rows, chan), F32),
                pltpu.VMEM((2 * rows * cols, chan), F32),
            ],
            flops=200_000_000 * len(steps),
            outside=range(len(wait)),
        )

    parts = [None] * chips
    for m, value in enumerate(partial_products(list(range(pieces, chips))), pieces):
        parts[m] = along_row(value, 2 * m)
    for m in reversed(range(pieces)):
        value = partial_products([m])[0]
        parts[m] = along_row(value, 2 * m) if m else value
    gate = call(gate_kernel, block32, [first, in_gating], flops=50_000_000)
    return call(last_kernel, block, parts + [first, gate, in_final], flops=100_000_000)


def solution(mesh):
    return jax.shard_map(
        functools.partial(on_device, mesh.shape["row"], mesh.shape["col"]),
        mesh=mesh,
        in_specs=(P(("groups", "row"), "col", None), P("groups"), P(), P(), P(), P(), P(), P()),
        out_specs=P(("groups", "row"), "col", None),
        check_vma=False,
    )
```

```python
import functools

import jax
import jax.numpy as jnp
from jax import lax
from jax.experimental import pallas as pl
from jax.experimental.pallas import tpu as pltpu
from jax.sharding import PartitionSpec as P

F32, BF16 = jnp.float32, jnp.bfloat16
VMEM = pl.BlockSpec(memory_space=pltpu.VMEM)
LIMIT = 40 * 1024 * 1024
FULL = 63 * 1024 * 1024


def after(kernel, count, *refs):
    kernel(*refs[count:])


def call(kernel, outs, args, scratch=(), flops=10_000_000, outside=(), limit=LIMIT):
    single = not isinstance(outs, (list, tuple))
    outs = [outs] if single else list(outs)
    moved = sum(a.size * a.dtype.itemsize for a in args) + sum(
        o.size * o.dtype.itemsize for o in outs
    )
    result = pl.pallas_call(
        kernel,
        out_shape=outs,
        in_specs=[
            pl.BlockSpec(memory_space=pl.ANY) if n in outside else VMEM for n in range(len(args))
        ],
        out_specs=[VMEM] * len(outs),
        scratch_shapes=list(scratch),
        compiler_params=pltpu.CompilerParams(vmem_limit_bytes=limit),
        cost_estimate=pl.CostEstimate(flops=flops, bytes_accessed=moved, transcendentals=0),
    )(*args)
    return result[0] if single else result


def shape(dims, dtype):
    return jax.ShapeDtypeStruct(dims, dtype)


def sigmoid(v):
    return 0.5 * jnp.tanh(0.5 * v) + 0.5


def layer_norm(v):
    center = jnp.mean(v, axis=-1, keepdims=True)
    shifted = v - center
    spread = jnp.mean(shifted * shifted, axis=-1, keepdims=True)
    return shifted * lax.rsqrt(spread + 1e-05)


def place():
    row = lax.axis_index("row")
    return row // 2, row % 2, lax.axis_index("col")


def token_weights(mask_row, start, count):
    tokens = mask_row.shape[1]
    lane = lax.broadcasted_iota(jnp.int32, (count, tokens), 1)
    row = lax.broadcasted_iota(jnp.int32, (count, tokens), 0)
    hot = jnp.where(lane == row + start, mask_row, 0.0).astype(BF16)
    return jnp.dot(hot, jnp.ones((tokens, 128), BF16), preferred_element_type=F32)


def gated(normed, w, mask_ref, rows, cols, x):
    hidden = w.shape[1] // 2
    projected = jnp.dot(normed, w, preferred_element_type=F32)
    value = sigmoid(projected[:, hidden:]) * projected[:, :hidden]
    mask_row = mask_ref[...].astype(F32)
    row_w = token_weights(mask_row, lax.axis_index("row") * rows, -(-rows // 8) * 8)
    col_w = token_weights(mask_row, x * cols, cols)
    weights = row_w[:rows, None, :] * col_w[None, :, :]
    return value * weights.reshape(rows * cols, 128)


def normed_of(pair):
    rows, cols, chan = pair.shape
    return layer_norm(pair.astype(F32)).astype(BF16).reshape(rows * cols, chan)


def opening_kernel(pair_hbm, mask_hbm, w_hbm, right_ref, pair_ref, mask_scr, w_scr, sems):
    rows, cols, chan = pair_ref.shape
    width = w_scr.shape[1]
    copies = [
        pltpu.make_async_copy(pair_hbm, pair_ref, sems.at[0]),
        pltpu.make_async_copy(w_hbm.at[:, pl.ds(width, width)], w_scr, sems.at[1]),
        pltpu.make_async_copy(mask_hbm, mask_scr, sems.at[2]),
    ]
    for copy in copies:
        copy.start()
    for copy in copies:
        copy.wait()
    value = gated(
        normed_of(pair_ref[...]), w_scr[...], mask_scr, rows, cols, lax.axis_index("col")
    )
    right_ref[...] = value.astype(BF16).reshape(right_ref.shape)


def left_kernel(pair_ref, mask_ref, w_ref, left_ref, copy_ref):
    rows, cols, _ = pair_ref.shape
    w = w_ref[:, : w_ref.shape[1] // 2]
    value = gated(normed_of(pair_ref[...]), w, mask_ref, rows, cols, lax.axis_index("col"))
    left_ref[...] = value.astype(BF16).reshape(left_ref.shape)
    copy_ref[...] = pair_ref[...]


def gates_kernel(cols_n, *refs):
    pairs, w_ref, outs = refs[:cols_n], refs[cols_n], refs[cols_n + 1 :]
    rows, cols, _ = pairs[0].shape
    pieces = cols // (2 * rows)
    z, _, x = place()
    for h in range(cols_n):
        pair_ref, gate_ref = outs[2 * h : 2 * h + 2]
        for dx in range(cols_n):

            @pl.when(((z // pieces) ^ x ^ h) == dx)
            def _():
                pair_ref[...] = pairs[dx][...]

        gate = jnp.dot(normed_of(pair_ref[...]), w_ref[...], preferred_element_type=F32)
        gate_ref[...] = sigmoid(gate).reshape(gate_ref.shape)


def gate_kernel(pair_ref, w_ref, gate_ref):
    gate = jnp.dot(normed_of(pair_ref[...]), w_ref[...], preferred_element_type=F32)
    gate_ref[...] = sigmoid(gate).reshape(gate_ref.shape)


def outgoing_kernel(carried, sides, *refs):
    earlier, lefts, refs = refs[:carried], refs[carried : carried + sides], refs[carried + sides :]
    rights, outs, (r_scr, l_scr, o_scr) = refs[: -3 - sides], refs[-3 - sides : -3], refs[-3:]
    rows, cols, chan = lefts[0].shape
    blocks = len(rights)
    used = blocks * rows
    width = -(-used // 8) * 8
    z, _, _ = place()
    for m, ref in enumerate(rights):
        base = ((z % blocks) ^ m) * rows
        for j in range(rows):
            r_scr[pl.ds(base + j, cols, stride=width), :] = ref[j].astype(F32)
    for n, (left, out_ref) in enumerate(zip(lefts, outs)):
        l_scr[...] = left[...].astype(F32).reshape(rows * cols, chan)

        def step(block, totals):
            for u in range(8):
                k = block * 8 + u
                right = r_scr[pl.ds(pl.multiple_of(k * width, 8), width), :]
                totals = tuple(
                    t + l_scr[pl.ds(i * cols + k, 1), :] * right for i, t in enumerate(totals)
                )
            return totals

        zero = jnp.zeros((width, chan), F32)
        totals = lax.fori_loop(0, cols // 8, step, (zero,) * rows)
        for i, t in enumerate(totals):
            o_scr[pl.ds(i * used, used), :] = t[:used]
        begin = out_ref.shape[0] - rows * used
        if carried:
            out_ref[pl.ds(0, begin), :] = earlier[n][...]
        out_ref[pl.ds(begin, rows * used), :] = o_scr[...].astype(BF16)


def first_kernel(cols_n, h, groups, *refs):
    parts, refs = refs[: 2 * cols_n * len(groups)], refs[2 * cols_n * len(groups) :]
    pair_ref, gate_ref, mask_ref, final_ref, w_ref = refs[:5]
    earlier, refs = refs[5:-6], refs[-6:]
    first_ref, right_ref, mine_ref, other_ref, scr, half_scr = refs
    rows, cols, chan = pair_ref.shape
    pieces = cols // (2 * rows)
    z, core, x = place()
    for n, (begin, start, count) in enumerate(groups):
        group = parts[2 * cols_n * n : 2 * cols_n * (n + 1)]
        size = rows * count * rows
        for some, side in ((group[:cols_n], core), (group[cols_n:], 1 - core)):
            value = some[0][pl.ds(begin, size), :].astype(F32)
            for ref in some[1:]:
                value = value + ref[pl.ds(begin, size), :].astype(F32)
            half_scr[pl.ds(0, size), :] = value
            for i in range(rows):
                for p in range(count):
                    q = p if count == pieces else (z % pieces) ^ start
                    part = half_scr[pl.ds((i * count + p) * rows, rows), :]
                    scr[pl.ds(i * cols + (2 * q + side) * rows, rows), :] = part
    mixed = layer_norm(scr[...]).astype(BF16)
    update = jnp.dot(mixed, final_ref[...], preferred_element_type=F32)
    pair = pair_ref[...].astype(F32).reshape(rows * cols, chan)
    first = (pair + gate_ref[...].reshape(rows * cols, chan) * update).astype(BF16)
    first_ref[...] = first.reshape(first_ref.shape)
    normed = layer_norm(first.astype(F32)).astype(BF16)
    width = w_ref.shape[1] // 2
    block = (z // pieces) ^ h
    scr[...] = gated(normed, w_ref[:, :width], mask_ref, rows, cols, block)
    for out_ref, side in ((mine_ref, core), (other_ref, 1 - core)):
        for i in range(rows):
            for q in range(pieces):
                part = scr[pl.ds(i * cols + (2 * q + side) * rows, rows), :]
                half_scr[pl.ds((i * pieces + q) * rows, rows), :] = part
        out_ref[...] = half_scr[...].astype(BF16).reshape(out_ref.shape)
    right = gated(normed, w_ref[:, width:], mask_ref, rows, cols, block)
    right_ref[...] = right.astype(BF16).reshape(right_ref.shape)
    for g in range(len(earlier) // 2):

        @pl.when(((z // pieces) ^ g) == x)
        def _():
            first_ref[...] = earlier[2 * g][...]
            right_ref[...] = earlier[2 * g + 1][...]


def incoming_kernel(steps, *refs):
    own_right, core_right = refs[:2]
    count = (len(refs) - 4 - len(steps)) // 2
    lefts = refs[2 : 2 + 2 * count]
    outs = refs[2 + 2 * count : -2]
    l_scr, r_scr = refs[-2:]
    rows, cols, chan = own_right.shape
    width = lefts[0].shape[1]
    pieces = width // rows
    z, _, _ = place()
    for n, ref in enumerate((own_right, core_right)):
        r_scr[pl.ds(n * rows * cols, rows * cols), :] = ref[...].astype(F32).reshape(-1, chan)
    for n, ref in enumerate(lefts):
        l_scr[pl.ds(n * rows * width, rows * width), :] = ref[...].astype(F32).reshape(-1, chan)
    for m, out_ref in zip(steps, outs):
        block = m // pieces - steps[0] // pieces
        base = block * (2 * rows * width) + ((z ^ m) % pieces) * rows
        for group in range(0, rows, 6):

            def step(k, totals):
                right = r_scr[pl.ds(pl.multiple_of(k * cols, 8), cols), :]
                return tuple(
                    t + l_scr[pl.ds(base + k * width + group + i, 1), :] * right
                    for i, t in enumerate(totals)
                )

            zero = jnp.zeros((cols, chan), F32)
            totals = lax.fori_loop(0, 2 * rows, step, (zero,) * 6, unroll=4)
            for i, t in enumerate(totals):
                out_ref[group + i] = t.astype(out_ref.dtype)


def last_kernel(*refs):
    parts, (first_ref, gate_ref, final_ref, out_ref) = refs[:-4], refs[-4:]
    rows, cols, chan = first_ref.shape
    product = parts[0][...].astype(F32)
    for ref in parts[1:]:
        product = product + ref[...].astype(F32)
    mixed = layer_norm(product).astype(BF16).reshape(rows * cols, chan)
    update = jnp.dot(mixed, final_ref[...], preferred_element_type=F32)
    first = first_ref[...].astype(F32).reshape(rows * cols, chan)
    result = first + gate_ref[...].reshape(rows * cols, chan) * update
    out_ref[...] = result.astype(BF16).reshape(out_ref.shape)


def on_device(
    rows_n,
    cols_n,
    pair_rep,
    token_mask,
    out_project,
    out_gating,
    out_final,
    in_project,
    in_gating,
    in_final,
):
    rows, cols, chan = pair_rep.shape
    chips = rows_n // 2
    pieces = cols // (2 * rows)
    mask = token_mask.reshape(1, -1)
    block = shape((rows, cols, chan), BF16)
    block32 = shape((rows, cols, chan), F32)
    half = (rows, pieces * rows, chan)

    def along_row(v, bits):
        return lax.ppermute(v, "row", [(i, i ^ bits) for i in range(rows_n)])

    def shift(v, dx, core):
        pairs = [
            (r * cols_n + c, (r ^ core) * cols_n + (c ^ dx))
            for r in range(rows_n)
            for c in range(cols_n)
        ]
        return lax.ppermute(v, ("row", "col"), pairs)

    right = call(
        opening_kernel,
        block,
        [pair_rep, mask, out_project],
        scratch=[
            pltpu.VMEM(pair_rep.shape, BF16),
            pltpu.VMEM(mask.shape, jnp.int32),
            pltpu.VMEM((chan, out_project.shape[1] // 2), BF16),
            pltpu.SemaphoreType.DMA((3,)),
        ],
        flops=100_000_000,
        outside=(0, 1, 2),
        limit=FULL,
    )
    rights = {0: right}
    bit = chips // 2
    while bit:
        for m in list(rights):
            rights[m | bit] = along_row(rights[m], 2 * bit)
        bit //= 2
    left, pair_copy = call(
        functools.partial(after, left_kernel, 1),
        [block, block],
        [right, pair_rep, mask, out_project],
        flops=100_000_000,
        outside=(0,),
    )
    pairs = [pair_copy] + [shift(pair_copy, dx, 0) for dx in range(1, cols_n)]
    core_left = along_row(left, 1)
    def product(blocks, sides, earlier=()):
        area = rows * len(blocks) * rows
        out = shape((area + sum(e.shape[0] for e in earlier[:1]), chan), BF16)
        return call(
            functools.partial(outgoing_kernel, len(earlier), len(sides)),
            [out] * len(sides),
            [*earlier, *sides] + [rights[m] for m in blocks],
            scratch=[
                pltpu.VMEM((cols * (-(-len(blocks) * rows // 8) * 8), chan), F32),
                pltpu.VMEM((rows * cols, chan), F32),
                pltpu.VMEM((area, chan), F32),
            ],
            flops=125_000_000 * len(blocks) * len(sides),
        )

    both = [left, core_left]
    early = []
    for h in range(cols_n - 1):
        early = product(range(h * pieces, (h + 1) * pieces), both, early)
    for m in range(chips - pieces, chips - 1):
        early = product([m], both, early)
    mine, other = early
    parts = [mine] + [shift(mine, dx, 0) for dx in range(1, cols_n)]
    across = [shift(other, dx, 1) for dx in range(1, cols_n)]
    other_core = other
    (mine,) = product([chips - 1], [left])
    mine, core_left = lax.optimization_barrier((mine, core_left))
    (other,) = product([chips - 1], [core_left])
    other, out_gating = lax.optimization_barrier((other, out_gating))
    gates = call(
        functools.partial(gates_kernel, cols_n),
        [block, block32] * cols_n,
        pairs + [out_gating],
        flops=100_000_000,
    )
    gates = list(gates)
    other_core, last_core, gates[1] = lax.optimization_barrier((other_core, other, gates[1]))
    exchanged = [parts + [shift(other_core, 0, 1)] + across]
    parts = [mine] + [shift(mine, dx, 0) for dx in range(1, cols_n)]
    parts += [shift(last_core, 0, 1)] + [shift(other, dx, 1) for dx in range(1, cols_n)]
    exchanged.append(parts)
    firsts, lefts = [], []
    for h in range(cols_n):
        area = rows * rows
        if h < cols_n - 1:
            groups, parts, earlier = [(h * pieces * area, 0, pieces)], exchanged[0], []
        else:
            groups = [((h * pieces + p) * area, p, 1) for p in range(pieces - 1)]
            groups.append((0, pieces - 1, 1))
            parts, earlier = exchanged[0] * (pieces - 1) + exchanged[1], firsts
        first, right, left_mine, left_other = call(
            functools.partial(first_kernel, cols_n, h, groups),
            [block, block, shape(half, BF16), shape(half, BF16)],
            parts + list(gates[2 * h : 2 * h + 2]) + [mask, out_final, in_project] + earlier,
            scratch=[
                pltpu.VMEM((rows * cols, chan), F32),
                pltpu.VMEM((rows * pieces * rows, chan), F32),
            ],
            flops=300_000_000,
        )
        firsts += [first, right]
        lefts.append([left_mine, along_row(left_other, 1)])

    core_right = along_row(right, 1)

    def partial_products(steps):
        used = lefts[steps[0] // pieces : steps[-1] // pieces + 1]
        wait = [] if used[-1] is lefts[-1] else lefts[-1]
        return call(
            functools.partial(after, functools.partial(incoming_kernel, steps), len(wait)),
            [block if m else block32 for m in steps],
            wait + [right, core_right] + sum(used, []),
            scratch=[
                pltpu.VMEM((2 * len(used) * rows * pieces * rows, chan), F32),
                pltpu.VMEM((2 * rows * cols, chan), F32),
            ],
            flops=200_000_000 * len(steps),
            outside=range(len(wait)),
        )

    parts = [None] * chips
    for m, value in enumerate(partial_products(list(range(pieces, chips))), pieces):
        parts[m] = along_row(value, 2 * m)
    for m in reversed(range(pieces)):
        value = partial_products([m])[0]
        parts[m] = along_row(value, 2 * m) if m else value
    gate = call(gate_kernel, block32, [first, in_gating], flops=50_000_000)
    return call(last_kernel, block, parts + [first, gate, in_final], flops=100_000_000)


def solution(mesh):
    return jax.shard_map(
        functools.partial(on_device, mesh.shape["row"], mesh.shape["col"]),
        mesh=mesh,
        in_specs=(P(("groups", "row"), "col", None), P("groups"), P(), P(), P(), P(), P(), P()),
        out_specs=P(("groups", "row"), "col", None),
        check_vma=False,
    )
```

```python
import functools

import jax
import jax.numpy as jnp
from jax import lax
from jax.experimental import pallas as pl
from jax.experimental.pallas import tpu as pltpu
from jax.sharding import PartitionSpec as P

F32, BF16 = jnp.float32, jnp.bfloat16
VMEM = pl.BlockSpec(memory_space=pltpu.VMEM)
LIMIT = 40 * 1024 * 1024
FULL = 63 * 1024 * 1024


def after(kernel, count, *refs):
    kernel(*refs[count:])


def call(kernel, outs, args, scratch=(), flops=10_000_000, outside=(), limit=LIMIT):
    single = not isinstance(outs, (list, tuple))
    outs = [outs] if single else list(outs)
    moved = sum(a.size * a.dtype.itemsize for a in args) + sum(
        o.size * o.dtype.itemsize for o in outs
    )
    result = pl.pallas_call(
        kernel,
        out_shape=outs,
        in_specs=[
            pl.BlockSpec(memory_space=pl.ANY) if n in outside else VMEM for n in range(len(args))
        ],
        out_specs=[VMEM] * len(outs),
        scratch_shapes=list(scratch),
        compiler_params=pltpu.CompilerParams(vmem_limit_bytes=limit),
        cost_estimate=pl.CostEstimate(flops=flops, bytes_accessed=moved, transcendentals=0),
    )(*args)
    return result[0] if single else result


def shape(dims, dtype):
    return jax.ShapeDtypeStruct(dims, dtype)


def sigmoid(v):
    return 0.5 * jnp.tanh(0.5 * v) + 0.5


def layer_norm(v):
    center = jnp.mean(v, axis=-1, keepdims=True)
    shifted = v - center
    spread = jnp.mean(shifted * shifted, axis=-1, keepdims=True)
    return shifted * lax.rsqrt(spread + 1e-05)


def place():
    row = lax.axis_index("row")
    return row // 2, row % 2, lax.axis_index("col")


def token_weights(mask_row, start, count):
    tokens = mask_row.shape[1]
    lane = lax.broadcasted_iota(jnp.int32, (count, tokens), 1)
    row = lax.broadcasted_iota(jnp.int32, (count, tokens), 0)
    hot = jnp.where(lane == row + start, mask_row, 0.0).astype(BF16)
    return jnp.dot(hot, jnp.ones((tokens, 128), BF16), preferred_element_type=F32)


def gated(normed, w, mask_ref, rows, cols, x):
    hidden = w.shape[1] // 2
    projected = jnp.dot(normed, w, preferred_element_type=F32)
    value = sigmoid(projected[:, hidden:]) * projected[:, :hidden]
    mask_row = mask_ref[...].astype(F32)
    row_w = token_weights(mask_row, lax.axis_index("row") * rows, -(-rows // 8) * 8)
    col_w = token_weights(mask_row, x * cols, cols)
    weights = row_w[:rows, None, :] * col_w[None, :, :]
    return value * weights.reshape(rows * cols, 128)


def normed_of(pair):
    rows, cols, chan = pair.shape
    return layer_norm(pair.astype(F32)).astype(BF16).reshape(rows * cols, chan)


def opening_kernel(pair_hbm, mask_hbm, w_hbm, right_ref, pair_ref, mask_scr, w_scr, sems):
    rows, cols, chan = pair_ref.shape
    width = w_scr.shape[1]
    copies = [
        pltpu.make_async_copy(pair_hbm, pair_ref, sems.at[0]),
        pltpu.make_async_copy(w_hbm.at[:, pl.ds(width, width)], w_scr, sems.at[1]),
        pltpu.make_async_copy(mask_hbm, mask_scr, sems.at[2]),
    ]
    for copy in copies:
        copy.start()
    for copy in copies:
        copy.wait()
    value = gated(
        normed_of(pair_ref[...]), w_scr[...], mask_scr, rows, cols, lax.axis_index("col")
    )
    right_ref[...] = value.astype(BF16).reshape(right_ref.shape)


def left_kernel(pair_ref, mask_ref, w_ref, left_ref, copy_ref):
    rows, cols, _ = pair_ref.shape
    w = w_ref[:, : w_ref.shape[1] // 2]
    value = gated(normed_of(pair_ref[...]), w, mask_ref, rows, cols, lax.axis_index("col"))
    left_ref[...] = value.astype(BF16).reshape(left_ref.shape)
    copy_ref[...] = pair_ref[...]


def gates_kernel(cols_n, *refs):
    pairs, w_ref, outs = refs[:cols_n], refs[cols_n], refs[cols_n + 1 :]
    rows, cols, _ = pairs[0].shape
    pieces = cols // (2 * rows)
    z, _, x = place()
    for h in range(cols_n):
        pair_ref, gate_ref = outs[2 * h : 2 * h + 2]
        for dx in range(cols_n):

            @pl.when(((z // pieces) ^ x ^ h) == dx)
            def _():
                pair_ref[...] = pairs[dx][...]

        gate = jnp.dot(normed_of(pair_ref[...]), w_ref[...], preferred_element_type=F32)
        gate_ref[...] = sigmoid(gate).reshape(gate_ref.shape)


def gate_kernel(pair_ref, w_ref, gate_ref):
    gate = jnp.dot(normed_of(pair_ref[...]), w_ref[...], preferred_element_type=F32)
    gate_ref[...] = sigmoid(gate).reshape(gate_ref.shape)


def outgoing_kernel(carried, sides, *refs):
    earlier, lefts, refs = refs[:carried], refs[carried : carried + sides], refs[carried + sides :]
    rights, outs, (r_scr, l_scr, o_scr) = refs[: -3 - sides], refs[-3 - sides : -3], refs[-3:]
    rows, cols, chan = lefts[0].shape
    blocks = len(rights)
    used = blocks * rows
    width = -(-used // 8) * 8
    z, _, _ = place()
    for m, ref in enumerate(rights):
        base = ((z % blocks) ^ m) * rows
        for j in range(rows):
            r_scr[pl.ds(base + j, cols, stride=width), :] = ref[j].astype(F32)
    for n, (left, out_ref) in enumerate(zip(lefts, outs)):
        l_scr[...] = left[...].astype(F32).reshape(rows * cols, chan)

        def step(block, totals):
            for u in range(8):
                k = block * 8 + u
                right = r_scr[pl.ds(pl.multiple_of(k * width, 8), width), :]
                totals = tuple(
                    t + l_scr[pl.ds(i * cols + k, 1), :] * right for i, t in enumerate(totals)
                )
            return totals

        zero = jnp.zeros((width, chan), F32)
        totals = lax.fori_loop(0, cols // 8, step, (zero,) * rows)
        for i, t in enumerate(totals):
            o_scr[pl.ds(i * used, used), :] = t[:used]
        begin = out_ref.shape[0] - rows * used
        if carried:
            out_ref[pl.ds(0, begin), :] = earlier[n][...]
        out_ref[pl.ds(begin, rows * used), :] = o_scr[...].astype(BF16)


def first_kernel(cols_n, h, groups, *refs):
    parts, refs = refs[: 2 * cols_n * len(groups)], refs[2 * cols_n * len(groups) :]
    pair_ref, gate_ref, mask_ref, final_ref, w_ref = refs[:5]
    earlier, refs = refs[5:-6], refs[-6:]
    first_ref, right_ref, mine_ref, other_ref, scr, half_scr = refs
    rows, cols, chan = pair_ref.shape
    pieces = cols // (2 * rows)
    z, core, x = place()
    for n, (begin, start, count) in enumerate(groups):
        group = parts[2 * cols_n * n : 2 * cols_n * (n + 1)]
        size = rows * count * rows
        for some, side in ((group[:cols_n], core), (group[cols_n:], 1 - core)):
            value = some[0][pl.ds(begin, size), :].astype(F32)
            for ref in some[1:]:
                value = value + ref[pl.ds(begin, size), :].astype(F32)
            half_scr[pl.ds(0, size), :] = value
            for i in range(rows):
                for p in range(count):
                    q = p if count == pieces else (z % pieces) ^ start
                    part = half_scr[pl.ds((i * count + p) * rows, rows), :]
                    scr[pl.ds(i * cols + (2 * q + side) * rows, rows), :] = part
    mixed = layer_norm(scr[...]).astype(BF16)
    update = jnp.dot(mixed, final_ref[...], preferred_element_type=F32)
    pair = pair_ref[...].astype(F32).reshape(rows * cols, chan)
    first = (pair + gate_ref[...].reshape(rows * cols, chan) * update).astype(BF16)
    first_ref[...] = first.reshape(first_ref.shape)
    normed = layer_norm(first.astype(F32)).astype(BF16)
    width = w_ref.shape[1] // 2
    block = (z // pieces) ^ h
    scr[...] = gated(normed, w_ref[:, :width], mask_ref, rows, cols, block)
    for out_ref, side in ((mine_ref, core), (other_ref, 1 - core)):
        for i in range(rows):
            for q in range(pieces):
                part = scr[pl.ds(i * cols + (2 * q + side) * rows, rows), :]
                half_scr[pl.ds((i * pieces + q) * rows, rows), :] = part
        out_ref[...] = half_scr[...].astype(BF16).reshape(out_ref.shape)
    right = gated(normed, w_ref[:, width:], mask_ref, rows, cols, block)
    right_ref[...] = right.astype(BF16).reshape(right_ref.shape)
    for g in range(len(earlier) // 2):

        @pl.when(((z // pieces) ^ g) == x)
        def _():
            first_ref[...] = earlier[2 * g][...]
            right_ref[...] = earlier[2 * g + 1][...]


def incoming_kernel(steps, *refs):
    own_right, core_right = refs[:2]
    count = (len(refs) - 4 - len(steps)) // 2
    lefts = refs[2 : 2 + 2 * count]
    outs = refs[2 + 2 * count : -2]
    l_scr, r_scr = refs[-2:]
    rows, cols, chan = own_right.shape
    width = lefts[0].shape[1]
    pieces = width // rows
    z, _, _ = place()
    for n, ref in enumerate((own_right, core_right)):
        r_scr[pl.ds(n * rows * cols, rows * cols), :] = ref[...].astype(F32).reshape(-1, chan)
    for n, ref in enumerate(lefts):
        l_scr[pl.ds(n * rows * width, rows * width), :] = ref[...].astype(F32).reshape(-1, chan)
    for m, out_ref in zip(steps, outs):
        block = m // pieces - steps[0] // pieces
        base = block * (2 * rows * width) + ((z ^ m) % pieces) * rows
        for group in range(0, rows, 6):

            def step(k, totals):
                right = r_scr[pl.ds(pl.multiple_of(k * cols, 8), cols), :]
                return tuple(
                    t + l_scr[pl.ds(base + k * width + group + i, 1), :] * right
                    for i, t in enumerate(totals)
                )

            zero = jnp.zeros((cols, chan), F32)
            totals = lax.fori_loop(0, 2 * rows, step, (zero,) * 6, unroll=4)
            for i, t in enumerate(totals):
                out_ref[group + i] = t.astype(out_ref.dtype)


def last_kernel(*refs):
    parts, (first_ref, gate_ref, final_ref, out_ref) = refs[:-4], refs[-4:]
    rows, cols, chan = first_ref.shape
    product = parts[0][...].astype(F32)
    for ref in parts[1:]:
        product = product + ref[...].astype(F32)
    mixed = layer_norm(product).astype(BF16).reshape(rows * cols, chan)
    update = jnp.dot(mixed, final_ref[...], preferred_element_type=F32)
    first = first_ref[...].astype(F32).reshape(rows * cols, chan)
    result = first + gate_ref[...].reshape(rows * cols, chan) * update
    out_ref[...] = result.astype(BF16).reshape(out_ref.shape)


def on_device(
    rows_n,
    cols_n,
    pair_rep,
    token_mask,
    out_project,
    out_gating,
    out_final,
    in_project,
    in_gating,
    in_final,
):
    rows, cols, chan = pair_rep.shape
    chips = rows_n // 2
    pieces = cols // (2 * rows)
    mask = token_mask.reshape(1, -1)
    block = shape((rows, cols, chan), BF16)
    block32 = shape((rows, cols, chan), F32)
    half = (rows, pieces * rows, chan)

    def along_row(v, bits):
        return lax.ppermute(v, "row", [(i, i ^ bits) for i in range(rows_n)])

    def shift(v, dx, core):
        pairs = [
            (r * cols_n + c, (r ^ core) * cols_n + (c ^ dx))
            for r in range(rows_n)
            for c in range(cols_n)
        ]
        return lax.ppermute(v, ("row", "col"), pairs)

    right = call(
        opening_kernel,
        block,
        [pair_rep, mask, out_project],
        scratch=[
            pltpu.VMEM(pair_rep.shape, BF16),
            pltpu.VMEM(mask.shape, jnp.int32),
            pltpu.VMEM((chan, out_project.shape[1] // 2), BF16),
            pltpu.SemaphoreType.DMA((3,)),
        ],
        flops=100_000_000,
        outside=(0, 1, 2),
        limit=FULL,
    )
    rights = {0: right}
    bit = chips // 2
    while bit:
        for m in list(rights):
            rights[m | bit] = along_row(rights[m], 2 * bit)
        bit //= 2
    left, pair_copy = call(
        functools.partial(after, left_kernel, 1),
        [block, block],
        [right, pair_rep, mask, out_project],
        flops=100_000_000,
        outside=(0,),
    )
    pairs = [pair_copy] + [shift(pair_copy, dx, 0) for dx in range(1, cols_n)]
    core_left = along_row(left, 1)
    def product(blocks, sides, earlier=()):
        area = rows * len(blocks) * rows
        out = shape((area + sum(e.shape[0] for e in earlier[:1]), chan), BF16)
        return call(
            functools.partial(outgoing_kernel, len(earlier), len(sides)),
            [out] * len(sides),
            [*earlier, *sides] + [rights[m] for m in blocks],
            scratch=[
                pltpu.VMEM((cols * (-(-len(blocks) * rows // 8) * 8), chan), F32),
                pltpu.VMEM((rows * cols, chan), F32),
                pltpu.VMEM((area, chan), F32),
            ],
            flops=125_000_000 * len(blocks) * len(sides),
        )

    both = [left, core_left]
    early = []
    for h in range(cols_n - 1):
        early = product(range(h * pieces, (h + 1) * pieces), both, early)
    for m in range(chips - pieces, chips - 1):
        early = product([m], both, early)
    mine, other = early
    parts = [mine] + [shift(mine, dx, 0) for dx in range(1, cols_n)]
    exchanged = [parts + [shift(other, dx, 1) for dx in range(cols_n)]]
    (mine,) = product([chips - 1], [left])
    mine, core_left = lax.optimization_barrier((mine, core_left))
    (other,) = product([chips - 1], [core_left])
    other, out_gating = lax.optimization_barrier((other, out_gating))
    gates = call(
        functools.partial(gates_kernel, cols_n),
        [block, block32] * cols_n,
        pairs + [out_gating],
        flops=100_000_000,
    )
    gates = list(gates)
    other_core, gates[1] = lax.optimization_barrier((other, gates[1]))
    parts = [mine] + [shift(mine, dx, 0) for dx in range(1, cols_n)]
    parts += [shift(other_core, 0, 1)] + [shift(other, dx, 1) for dx in range(1, cols_n)]
    exchanged.append(parts)
    firsts, lefts = [], []
    for h in range(cols_n):
        area = rows * rows
        if h < cols_n - 1:
            groups, parts, earlier = [(h * pieces * area, 0, pieces)], exchanged[0], []
        else:
            groups = [((h * pieces + p) * area, p, 1) for p in range(pieces - 1)]
            groups.append((0, pieces - 1, 1))
            parts, earlier = exchanged[0] * (pieces - 1) + exchanged[1], firsts
        first, right, left_mine, left_other = call(
            functools.partial(first_kernel, cols_n, h, groups),
            [block, block, shape(half, BF16), shape(half, BF16)],
            parts + list(gates[2 * h : 2 * h + 2]) + [mask, out_final, in_project] + earlier,
            scratch=[
                pltpu.VMEM((rows * cols, chan), F32),
                pltpu.VMEM((rows * pieces * rows, chan), F32),
            ],
            flops=300_000_000,
        )
        firsts += [first, right]
        lefts.append([left_mine, along_row(left_other, 1)])

    core_right = along_row(right, 1)

    def partial_products(steps):
        used = lefts[steps[0] // pieces : steps[-1] // pieces + 1]
        wait = [] if used[-1] is lefts[-1] else lefts[-1]
        return call(
            functools.partial(after, functools.partial(incoming_kernel, steps), len(wait)),
            [block if m else block32 for m in steps],
            wait + [right, core_right] + sum(used, []),
            scratch=[
                pltpu.VMEM((2 * len(used) * rows * pieces * rows, chan), F32),
                pltpu.VMEM((2 * rows * cols, chan), F32),
            ],
            flops=200_000_000 * len(steps),
            outside=range(len(wait)),
        )

    parts = [None] * chips
    for m, value in enumerate(partial_products(list(range(pieces, chips))), pieces):
        parts[m] = along_row(value, 2 * m)
    for m in reversed(range(pieces)):
        value = partial_products([m])[0]
        parts[m] = along_row(value, 2 * m) if m else value
    gate = call(gate_kernel, block32, [first, in_gating], flops=50_000_000)
    return call(last_kernel, block, parts + [first, gate, in_final], flops=100_000_000)


def solution(mesh):
    return jax.shard_map(
        functools.partial(on_device, mesh.shape["row"], mesh.shape["col"]),
        mesh=mesh,
        in_specs=(P(("groups", "row"), "col", None), P("groups"), P(), P(), P(), P(), P(), P()),
        out_specs=P(("groups", "row"), "col", None),
        check_vma=False,
    )
```

```python
import functools

import jax
import jax.numpy as jnp
from jax import lax
from jax.experimental import pallas as pl
from jax.experimental.pallas import tpu as pltpu
from jax.sharding import PartitionSpec as P

F32, BF16 = jnp.float32, jnp.bfloat16
VMEM = pl.BlockSpec(memory_space=pltpu.VMEM)
LIMIT = 40 * 1024 * 1024
FULL = 63 * 1024 * 1024


def after(kernel, count, *refs):
    kernel(*refs[count:])


def call(kernel, outs, args, scratch=(), flops=10_000_000, outside=(), limit=LIMIT):
    single = not isinstance(outs, (list, tuple))
    outs = [outs] if single else list(outs)
    moved = sum(a.size * a.dtype.itemsize for a in args) + sum(
        o.size * o.dtype.itemsize for o in outs
    )
    result = pl.pallas_call(
        kernel,
        out_shape=outs,
        in_specs=[
            pl.BlockSpec(memory_space=pl.ANY) if n in outside else VMEM for n in range(len(args))
        ],
        out_specs=[VMEM] * len(outs),
        scratch_shapes=list(scratch),
        compiler_params=pltpu.CompilerParams(vmem_limit_bytes=limit),
        cost_estimate=pl.CostEstimate(flops=flops, bytes_accessed=moved, transcendentals=0),
    )(*args)
    return result[0] if single else result


def shape(dims, dtype):
    return jax.ShapeDtypeStruct(dims, dtype)


def sigmoid(v):
    return 0.5 * jnp.tanh(0.5 * v) + 0.5


def layer_norm(v):
    center = jnp.mean(v, axis=-1, keepdims=True)
    shifted = v - center
    spread = jnp.mean(shifted * shifted, axis=-1, keepdims=True)
    return shifted * lax.rsqrt(spread + 1e-05)


def place():
    row = lax.axis_index("row")
    return row // 2, row % 2, lax.axis_index("col")


def token_weights(mask_row, start, count):
    tokens = mask_row.shape[1]
    lane = lax.broadcasted_iota(jnp.int32, (count, tokens), 1)
    row = lax.broadcasted_iota(jnp.int32, (count, tokens), 0)
    hot = jnp.where(lane == row + start, mask_row, 0.0).astype(BF16)
    return jnp.dot(hot, jnp.ones((tokens, 128), BF16), preferred_element_type=F32)


def gated(normed, w, mask_ref, rows, cols, x):
    hidden = w.shape[1] // 2
    projected = jnp.dot(normed, w, preferred_element_type=F32)
    value = sigmoid(projected[:, hidden:]) * projected[:, :hidden]
    mask_row = mask_ref[...].astype(F32)
    row_w = token_weights(mask_row, lax.axis_index("row") * rows, -(-rows // 8) * 8)
    col_w = token_weights(mask_row, x * cols, cols)
    weights = row_w[:rows, None, :] * col_w[None, :, :]
    return value * weights.reshape(rows * cols, 128)


def normed_of(pair):
    rows, cols, chan = pair.shape
    return layer_norm(pair.astype(F32)).astype(BF16).reshape(rows * cols, chan)


def opening_kernel(pair_hbm, mask_hbm, w_hbm, right_ref, pair_ref, mask_scr, w_scr, sems):
    rows, cols, chan = pair_ref.shape
    width = w_scr.shape[1]
    copies = [
        pltpu.make_async_copy(pair_hbm, pair_ref, sems.at[0]),
        pltpu.make_async_copy(w_hbm.at[:, pl.ds(width, width)], w_scr, sems.at[1]),
        pltpu.make_async_copy(mask_hbm, mask_scr, sems.at[2]),
    ]
    for copy in copies:
        copy.start()
    for copy in copies:
        copy.wait()
    value = gated(
        normed_of(pair_ref[...]), w_scr[...], mask_scr, rows, cols, lax.axis_index("col")
    )
    right_ref[...] = value.astype(BF16).reshape(right_ref.shape)


def left_kernel(pair_ref, mask_ref, w_ref, left_ref, copy_ref):
    rows, cols, _ = pair_ref.shape
    w = w_ref[:, : w_ref.shape[1] // 2]
    value = gated(normed_of(pair_ref[...]), w, mask_ref, rows, cols, lax.axis_index("col"))
    left_ref[...] = value.astype(BF16).reshape(left_ref.shape)
    copy_ref[...] = pair_ref[...]


def gates_kernel(cols_n, *refs):
    pairs, w_ref, outs = refs[:cols_n], refs[cols_n], refs[cols_n + 1 :]
    rows, cols, _ = pairs[0].shape
    pieces = cols // (2 * rows)
    z, _, x = place()
    for h in range(cols_n):
        pair_ref, gate_ref = outs[2 * h : 2 * h + 2]
        for dx in range(cols_n):

            @pl.when(((z // pieces) ^ x ^ h) == dx)
            def _():
                pair_ref[...] = pairs[dx][...]

        gate = jnp.dot(normed_of(pair_ref[...]), w_ref[...], preferred_element_type=F32)
        gate_ref[...] = sigmoid(gate).reshape(gate_ref.shape)


def gate_kernel(pair_ref, w_ref, gate_ref):
    gate = jnp.dot(normed_of(pair_ref[...]), w_ref[...], preferred_element_type=F32)
    gate_ref[...] = sigmoid(gate).reshape(gate_ref.shape)


def outgoing_kernel(carried, sides, *refs):
    earlier, lefts, refs = refs[:carried], refs[carried : carried + sides], refs[carried + sides :]
    rights, outs, (r_scr, l_scr, o_scr) = refs[: -3 - sides], refs[-3 - sides : -3], refs[-3:]
    rows, cols, chan = lefts[0].shape
    blocks = len(rights)
    used = blocks * rows
    width = -(-used // 8) * 8
    z, _, _ = place()
    for m, ref in enumerate(rights):
        base = ((z % blocks) ^ m) * rows
        for j in range(rows):
            r_scr[pl.ds(base + j, cols, stride=width), :] = ref[j].astype(F32)
    for n, (left, out_ref) in enumerate(zip(lefts, outs)):
        l_scr[...] = left[...].astype(F32).reshape(rows * cols, chan)

        def step(block, totals):
            for u in range(8):
                k = block * 8 + u
                right = r_scr[pl.ds(pl.multiple_of(k * width, 8), width), :]
                totals = tuple(
                    t + l_scr[pl.ds(i * cols + k, 1), :] * right for i, t in enumerate(totals)
                )
            return totals

        zero = jnp.zeros((width, chan), F32)
        totals = lax.fori_loop(0, cols // 8, step, (zero,) * rows)
        for i, t in enumerate(totals):
            o_scr[pl.ds(i * used, used), :] = t[:used]
        begin = out_ref.shape[0] - rows * used
        if carried:
            out_ref[pl.ds(0, begin), :] = earlier[n][...]
        out_ref[pl.ds(begin, rows * used), :] = o_scr[...].astype(BF16)


def first_kernel(cols_n, h, groups, *refs):
    parts, refs = refs[: 2 * cols_n * len(groups)], refs[2 * cols_n * len(groups) :]
    pair_ref, gate_ref, mask_ref, final_ref, w_ref = refs[:5]
    earlier, refs = refs[5:-6], refs[-6:]
    first_ref, right_ref, mine_ref, other_ref, scr, half_scr = refs
    rows, cols, chan = pair_ref.shape
    pieces = cols // (2 * rows)
    z, core, x = place()
    for n, (begin, start, count) in enumerate(groups):
        group = parts[2 * cols_n * n : 2 * cols_n * (n + 1)]
        size = rows * count * rows
        for some, side in ((group[:cols_n], core), (group[cols_n:], 1 - core)):
            value = some[0][pl.ds(begin, size), :].astype(F32)
            for ref in some[1:]:
                value = value + ref[pl.ds(begin, size), :].astype(F32)
            half_scr[pl.ds(0, size), :] = value
            for i in range(rows):
                for p in range(count):
                    q = p if count == pieces else (z % pieces) ^ start
                    part = half_scr[pl.ds((i * count + p) * rows, rows), :]
                    scr[pl.ds(i * cols + (2 * q + side) * rows, rows), :] = part
    mixed = layer_norm(scr[...]).astype(BF16)
    update = jnp.dot(mixed, final_ref[...], preferred_element_type=F32)
    pair = pair_ref[...].astype(F32).reshape(rows * cols, chan)
    first = (pair + gate_ref[...].reshape(rows * cols, chan) * update).astype(BF16)
    first_ref[...] = first.reshape(first_ref.shape)
    normed = layer_norm(first.astype(F32)).astype(BF16)
    width = w_ref.shape[1] // 2
    block = (z // pieces) ^ h
    scr[...] = gated(normed, w_ref[:, :width], mask_ref, rows, cols, block)
    for out_ref, side in ((mine_ref, core), (other_ref, 1 - core)):
        for i in range(rows):
            for q in range(pieces):
                part = scr[pl.ds(i * cols + (2 * q + side) * rows, rows), :]
                half_scr[pl.ds((i * pieces + q) * rows, rows), :] = part
        out_ref[...] = half_scr[...].astype(BF16).reshape(out_ref.shape)
    right = gated(normed, w_ref[:, width:], mask_ref, rows, cols, block)
    right_ref[...] = right.astype(BF16).reshape(right_ref.shape)
    for g in range(len(earlier) // 2):

        @pl.when(((z // pieces) ^ g) == x)
        def _():
            first_ref[...] = earlier[2 * g][...]
            right_ref[...] = earlier[2 * g + 1][...]


def incoming_kernel(steps, *refs):
    outs, (l_scr, r_scr) = refs[-2 - len(steps) : -2], refs[-2:]
    own_right, core_right, *lefts = refs[: -2 - len(steps)]
    rows, cols, chan = own_right.shape
    width = lefts[0].shape[1]
    pieces = width // rows
    z, _, _ = place()
    for n, ref in enumerate((own_right, core_right)):
        r_scr[pl.ds(n * rows * cols, rows * cols), :] = ref[...].astype(F32).reshape(-1, chan)
    for n, ref in enumerate(lefts):
        l_scr[pl.ds(n * rows * width, rows * width), :] = ref[...].astype(F32).reshape(-1, chan)
    for (m, begin, count), out_ref in zip(steps, outs):
        block = m // pieces - steps[0][0] // pieces
        base = block * (2 * rows * width) + ((z ^ m) % pieces) * rows + begin
        for group in range(0, count, 6):

            def step(k, totals):
                right = r_scr[pl.ds(pl.multiple_of(k * cols, 8), cols), :]
                return tuple(
                    t + l_scr[pl.ds(base + k * width + group + i, 1), :] * right
                    for i, t in enumerate(totals)
                )

            zero = jnp.zeros((cols, chan), F32)
            totals = lax.fori_loop(0, 2 * rows, step, (zero,) * min(6, count - group), unroll=4)
            for i, t in enumerate(totals):
                out_ref[group + i] = t.astype(out_ref.dtype)


def last_kernel(whole, upper, *refs):
    parts, (first_ref, gate_ref, final_ref, out_ref) = refs[:-4], refs[-4:]
    rows, cols, chan = first_ref.shape
    product = sum(ref[...].astype(F32) for ref in parts[:whole])
    top = sum(ref[...].astype(F32) for ref in parts[whole : whole + upper])
    low = sum(ref[...].astype(F32) for ref in parts[whole + upper :])
    product = product + jnp.concatenate([top, low], axis=0)
    mixed = layer_norm(product).astype(BF16).reshape(rows * cols, chan)
    update = jnp.dot(mixed, final_ref[...], preferred_element_type=F32)
    first = first_ref[...].astype(F32).reshape(rows * cols, chan)
    result = first + gate_ref[...].reshape(rows * cols, chan) * update
    out_ref[...] = result.astype(BF16).reshape(out_ref.shape)


def on_device(
    rows_n,
    cols_n,
    pair_rep,
    token_mask,
    out_project,
    out_gating,
    out_final,
    in_project,
    in_gating,
    in_final,
):
    rows, cols, chan = pair_rep.shape
    chips = rows_n // 2
    pieces = cols // (2 * rows)
    mask = token_mask.reshape(1, -1)
    block = shape((rows, cols, chan), BF16)
    block32 = shape((rows, cols, chan), F32)
    half = (rows, pieces * rows, chan)

    def along_row(v, bits):
        return lax.ppermute(v, "row", [(i, i ^ bits) for i in range(rows_n)])

    def shift(v, dx, core):
        pairs = [
            (r * cols_n + c, (r ^ core) * cols_n + (c ^ dx))
            for r in range(rows_n)
            for c in range(cols_n)
        ]
        return lax.ppermute(v, ("row", "col"), pairs)

    right = call(
        opening_kernel,
        block,
        [pair_rep, mask, out_project],
        scratch=[
            pltpu.VMEM(pair_rep.shape, BF16),
            pltpu.VMEM(mask.shape, jnp.int32),
            pltpu.VMEM((chan, out_project.shape[1] // 2), BF16),
            pltpu.SemaphoreType.DMA((3,)),
        ],
        flops=100_000_000,
        outside=(0, 1, 2),
        limit=FULL,
    )
    rights = {0: right}
    bit = chips // 2
    while bit:
        for m in list(rights):
            rights[m | bit] = along_row(rights[m], 2 * bit)
        bit //= 2
    left, pair_copy = call(
        functools.partial(after, left_kernel, 1),
        [block, block],
        [right, pair_rep, mask, out_project],
        flops=100_000_000,
        outside=(0,),
    )
    pairs = [pair_copy] + [shift(pair_copy, dx, 0) for dx in range(1, cols_n)]
    core_left = along_row(left, 1)
    def product(blocks, sides, earlier=()):
        area = rows * len(blocks) * rows
        out = shape((area + sum(e.shape[0] for e in earlier[:1]), chan), BF16)
        return call(
            functools.partial(outgoing_kernel, len(earlier), len(sides)),
            [out] * len(sides),
            [*earlier, *sides] + [rights[m] for m in blocks],
            scratch=[
                pltpu.VMEM((cols * (-(-len(blocks) * rows // 8) * 8), chan), F32),
                pltpu.VMEM((rows * cols, chan), F32),
                pltpu.VMEM((area, chan), F32),
            ],
            flops=125_000_000 * len(blocks) * len(sides),
        )

    both = [left, core_left]
    early = []
    for h in range(cols_n - 1):
        early = product(range(h * pieces, (h + 1) * pieces), both, early)
    for m in range(chips - pieces, chips - 1):
        early = product([m], both, early)
    mine, other = early
    parts = [mine] + [shift(mine, dx, 0) for dx in range(1, cols_n)]
    exchanged = [parts + [shift(other, dx, 1) for dx in range(cols_n)]]
    (mine,) = product([chips - 1], [left])
    mine, core_left = lax.optimization_barrier((mine, core_left))
    (other,) = product([chips - 1], [core_left])
    other, out_gating = lax.optimization_barrier((other, out_gating))
    gates = call(
        functools.partial(gates_kernel, cols_n),
        [block, block32] * cols_n,
        pairs + [out_gating],
        flops=100_000_000,
    )
    gates = list(gates)
    other_core, gates[1] = lax.optimization_barrier((other, gates[1]))
    parts = [mine] + [shift(mine, dx, 0) for dx in range(1, cols_n)]
    parts += [shift(other_core, 0, 1)] + [shift(other, dx, 1) for dx in range(1, cols_n)]
    exchanged.append(parts)
    firsts, lefts = [], []
    for h in range(cols_n):
        area = rows * rows
        if h < cols_n - 1:
            groups, parts, earlier = [(h * pieces * area, 0, pieces)], exchanged[0], []
        else:
            groups = [((h * pieces + p) * area, p, 1) for p in range(pieces - 1)]
            groups.append((0, pieces - 1, 1))
            parts, earlier = exchanged[0] * (pieces - 1) + exchanged[1], firsts
        first, right, left_mine, left_other = call(
            functools.partial(first_kernel, cols_n, h, groups),
            [block, block, shape(half, BF16), shape(half, BF16)],
            parts + list(gates[2 * h : 2 * h + 2]) + [mask, out_final, in_project] + earlier,
            scratch=[
                pltpu.VMEM((rows * cols, chan), F32),
                pltpu.VMEM((rows * pieces * rows, chan), F32),
            ],
            flops=300_000_000,
        )
        firsts += [first, right]
        lefts.append([left_mine, along_row(left_other, 1)])

    core_right = along_row(right, 1)

    def partial_products(steps):
        used = lefts[steps[0][0] // pieces : steps[-1][0] // pieces + 1]
        wait = [] if used[-1] is lefts[-1] else lefts[-1]
        return call(
            functools.partial(after, functools.partial(incoming_kernel, steps), len(wait)),
            [shape((count, cols, chan), BF16 if m else F32) for m, _, count in steps],
            wait + [right, core_right] + sum(used, []),
            scratch=[
                pltpu.VMEM((2 * len(used) * rows * pieces * rows, chan), F32),
                pltpu.VMEM((2 * rows * cols, chan), F32),
            ],
            flops=20_000_000 * sum(count for *_, count in steps),
            outside=range(len(wait)),
        )

    cut = rows // 2
    top, low = [], []
    for h in range(1, cols_n):
        blocks = range(h * pieces, (h + 1) * pieces)
        relayed = partial_products([(m, cut, rows - cut) for m in blocks[1:]])
        relayed = [along_row(v, 2 * p) for p, v in enumerate(relayed, 1)]
        *direct, own = partial_products(
            [(m, 0, cut) for m in blocks] + [(blocks[0], cut, rows - cut)]
        )
        top += [along_row(v, 2 * m) for m, v in zip(blocks, direct)]
        total = sum((v.astype(F32) for v in relayed), own.astype(F32)).astype(BF16)
        low.append(along_row(total, 2 * blocks[0]))
    near = [partial_products([(m, 0, rows)])[0] for m in range(pieces)]
    near = [along_row(v, 2 * m) if m else v for m, v in enumerate(near)]
    gate = call(gate_kernel, block32, [first, in_gating], flops=50_000_000)
    return call(
        functools.partial(last_kernel, len(near), len(top)),
        block,
        near + top + low + [first, gate, in_final],
        flops=100_000_000,
    )


def solution(mesh):
    return jax.shard_map(
        functools.partial(on_device, mesh.shape["row"], mesh.shape["col"]),
        mesh=mesh,
        in_specs=(P(("groups", "row"), "col", None), P("groups"), P(), P(), P(), P(), P(), P()),
        out_specs=P(("groups", "row"), "col", None),
        check_vma=False,
    )
```

```python
import functools

import jax
import jax.numpy as jnp
from jax import lax
from jax.experimental import pallas as pl
from jax.experimental.pallas import tpu as pltpu
from jax.sharding import PartitionSpec as P

F32, BF16 = jnp.float32, jnp.bfloat16
VMEM = pl.BlockSpec(memory_space=pltpu.VMEM)
LIMIT = 40 * 1024 * 1024


def after(kernel, count, *refs):
    kernel(*refs[count:])


def call(kernel, outs, args, scratch=(), flops=10_000_000, outside=(), limit=LIMIT):
    single = not isinstance(outs, (list, tuple))
    outs = [outs] if single else list(outs)
    moved = sum(a.size * a.dtype.itemsize for a in args) + sum(
        o.size * o.dtype.itemsize for o in outs
    )
    result = pl.pallas_call(
        kernel,
        out_shape=outs,
        in_specs=[
            pl.BlockSpec(memory_space=pl.ANY) if n in outside else VMEM for n in range(len(args))
        ],
        out_specs=[VMEM] * len(outs),
        scratch_shapes=list(scratch),
        compiler_params=pltpu.CompilerParams(vmem_limit_bytes=limit),
        cost_estimate=pl.CostEstimate(flops=flops, bytes_accessed=moved, transcendentals=0),
    )(*args)
    return result[0] if single else result


def shape(dims, dtype):
    return jax.ShapeDtypeStruct(dims, dtype)


def sigmoid(v):
    return 0.5 * jnp.tanh(0.5 * v) + 0.5


def layer_norm(v):
    center = jnp.mean(v, axis=-1, keepdims=True)
    shifted = v - center
    spread = jnp.mean(shifted * shifted, axis=-1, keepdims=True)
    return shifted * lax.rsqrt(spread + 1e-05)


def place():
    row = lax.axis_index("row")
    return row // 2, row % 2, lax.axis_index("col")


def token_weights(mask_row, start, count):
    tokens = mask_row.shape[1]
    lane = lax.broadcasted_iota(jnp.int32, (count, tokens), 1)
    row = lax.broadcasted_iota(jnp.int32, (count, tokens), 0)
    hot = jnp.where(lane == row + start, mask_row, 0.0).astype(BF16)
    return jnp.dot(hot, jnp.ones((tokens, 128), BF16), preferred_element_type=F32)


def gated(normed, w, mask_ref, rows, cols, x):
    hidden = w.shape[1] // 2
    projected = jnp.dot(normed, w, preferred_element_type=F32)
    value = sigmoid(projected[:, hidden:]) * projected[:, :hidden]
    mask_row = mask_ref[...].astype(F32)
    row_w = token_weights(mask_row, lax.axis_index("row") * rows, -(-rows // 8) * 8)
    col_w = token_weights(mask_row, x * cols, cols)
    weights = row_w[:rows, None, :] * col_w[None, :, :]
    return value * weights.reshape(rows * cols, 128)


def normed_of(pair):
    rows, cols, chan = pair.shape
    return layer_norm(pair.astype(F32)).astype(BF16).reshape(rows * cols, chan)


def opening_kernel(pair_hbm, mask_hbm, w_hbm, right_ref, pair_ref, mask_scr, w_scr, sems):
    rows, cols, chan = pair_ref.shape
    width = w_scr.shape[1]
    copies = [
        pltpu.make_async_copy(pair_hbm, pair_ref, sems.at[0]),
        pltpu.make_async_copy(w_hbm.at[:, pl.ds(width, width)], w_scr, sems.at[1]),
        pltpu.make_async_copy(mask_hbm, mask_scr, sems.at[2]),
    ]
    for copy in copies:
        copy.start()
    for copy in copies:
        copy.wait()
    value = gated(
        normed_of(pair_ref[...]), w_scr[...], mask_scr, rows, cols, lax.axis_index("col")
    )
    right_ref[...] = value.astype(BF16).reshape(right_ref.shape)


def left_kernel(pair_ref, mask_ref, w_ref, left_ref, copy_ref):
    rows, cols, _ = pair_ref.shape
    w = w_ref[:, : w_ref.shape[1] // 2]
    value = gated(normed_of(pair_ref[...]), w, mask_ref, rows, cols, lax.axis_index("col"))
    left_ref[...] = value.astype(BF16).reshape(left_ref.shape)
    copy_ref[...] = pair_ref[...]


def gates_kernel(cols_n, *refs):
    pairs, w_ref, outs = refs[:cols_n], refs[cols_n], refs[cols_n + 1 :]
    rows, cols, _ = pairs[0].shape
    pieces = cols // (2 * rows)
    z, _, x = place()
    for h in range(cols_n):
        pair_ref, gate_ref = outs[2 * h : 2 * h + 2]
        for dx in range(cols_n):

            @pl.when(((z // pieces) ^ x ^ h) == dx)
            def _():
                pair_ref[...] = pairs[dx][...]

        gate = jnp.dot(normed_of(pair_ref[...]), w_ref[...], preferred_element_type=F32)
        gate_ref[...] = sigmoid(gate).reshape(gate_ref.shape)


def gate_kernel(pair_ref, w_ref, gate_ref):
    gate = jnp.dot(normed_of(pair_ref[...]), w_ref[...], preferred_element_type=F32)
    gate_ref[...] = sigmoid(gate).reshape(gate_ref.shape)


def outgoing_kernel(carried, sides, *refs):
    earlier, lefts, refs = refs[:carried], refs[carried : carried + sides], refs[carried + sides :]
    rights, outs, (r_scr, l_scr, o_scr) = refs[: -3 - sides], refs[-3 - sides : -3], refs[-3:]
    rows, cols, chan = lefts[0].shape
    blocks = len(rights)
    used = blocks * rows
    width = -(-used // 8) * 8
    z, _, _ = place()
    for m, ref in enumerate(rights):
        base = ((z % blocks) ^ m) * rows
        for j in range(rows):
            r_scr[pl.ds(base + j, cols, stride=width), :] = ref[j].astype(F32)
    for n, (left, out_ref) in enumerate(zip(lefts, outs)):
        l_scr[...] = left[...].astype(F32).reshape(rows * cols, chan)

        def step(block, totals):
            for u in range(8):
                k = block * 8 + u
                right = r_scr[pl.ds(pl.multiple_of(k * width, 8), width), :]
                totals = tuple(
                    t + l_scr[pl.ds(i * cols + k, 1), :] * right for i, t in enumerate(totals)
                )
            return totals

        zero = jnp.zeros((width, chan), F32)
        totals = lax.fori_loop(0, cols // 8, step, (zero,) * rows)
        for i, t in enumerate(totals):
            o_scr[pl.ds(i * used, used), :] = t[:used]
        begin = out_ref.shape[0] - rows * used
        if carried:
            out_ref[pl.ds(0, begin), :] = earlier[n][...]
        out_ref[pl.ds(begin, rows * used), :] = o_scr[...].astype(BF16)


def first_kernel(cols_n, h, groups, *refs):
    parts, refs = refs[: 2 * cols_n * len(groups)], refs[2 * cols_n * len(groups) :]
    pair_ref, gate_ref, mask_ref, final_ref, w_ref = refs[:5]
    earlier, refs = refs[5:-6], refs[-6:]
    first_ref, right_ref, mine_ref, other_ref, scr, half_scr = refs
    rows, cols, chan = pair_ref.shape
    pieces = cols // (2 * rows)
    z, core, x = place()
    for n, (begin, start, count) in enumerate(groups):
        group = parts[2 * cols_n * n : 2 * cols_n * (n + 1)]
        size = rows * count * rows
        for some, side in ((group[:cols_n], core), (group[cols_n:], 1 - core)):
            value = some[0][pl.ds(begin, size), :].astype(F32)
            for ref in some[1:]:
                value = value + ref[pl.ds(begin, size), :].astype(F32)
            half_scr[pl.ds(0, size), :] = value
            for i in range(rows):
                for p in range(count):
                    q = p if count == pieces else (z % pieces) ^ start
                    part = half_scr[pl.ds((i * count + p) * rows, rows), :]
                    scr[pl.ds(i * cols + (2 * q + side) * rows, rows), :] = part
    mixed = layer_norm(scr[...]).astype(BF16)
    update = jnp.dot(mixed, final_ref[...], preferred_element_type=F32)
    pair = pair_ref[...].astype(F32).reshape(rows * cols, chan)
    first = (pair + gate_ref[...].reshape(rows * cols, chan) * update).astype(BF16)
    first_ref[...] = first.reshape(first_ref.shape)
    normed = layer_norm(first.astype(F32)).astype(BF16)
    width = w_ref.shape[1] // 2
    block = (z // pieces) ^ h
    scr[...] = gated(normed, w_ref[:, :width], mask_ref, rows, cols, block)
    for out_ref, side in ((mine_ref, core), (other_ref, 1 - core)):
        for i in range(rows):
            for q in range(pieces):
                part = scr[pl.ds(i * cols + (2 * q + side) * rows, rows), :]
                half_scr[pl.ds((i * pieces + q) * rows, rows), :] = part
        out_ref[...] = half_scr[...].astype(BF16).reshape(out_ref.shape)
    right = gated(normed, w_ref[:, width:], mask_ref, rows, cols, block)
    right_ref[...] = right.astype(BF16).reshape(right_ref.shape)
    for g in range(len(earlier) // 2):

        @pl.when(((z // pieces) ^ g) == x)
        def _():
            first_ref[...] = earlier[2 * g][...]
            right_ref[...] = earlier[2 * g + 1][...]


def incoming_kernel(steps, *refs):
    outs, (l_scr, r_scr) = refs[-2 - len(steps) : -2], refs[-2:]
    own_right, core_right, *lefts = refs[: -2 - len(steps)]
    rows, cols, chan = own_right.shape
    width = lefts[0].shape[1]
    pieces = width // rows
    z, _, _ = place()
    for n, ref in enumerate((own_right, core_right)):
        r_scr[pl.ds(n * rows * cols, rows * cols), :] = ref[...].astype(F32).reshape(-1, chan)
    for n, ref in enumerate(lefts):
        l_scr[pl.ds(n * rows * width, rows * width), :] = ref[...].astype(F32).reshape(-1, chan)
    for (m, begin, count), out_ref in zip(steps, outs):
        block = m // pieces - steps[0][0] // pieces
        base = block * (2 * rows * width) + ((z ^ m) % pieces) * rows + begin
        for group in range(0, count, 6):

            def step(k, totals):
                right = r_scr[pl.ds(pl.multiple_of(k * cols, 8), cols), :]
                return tuple(
                    t + l_scr[pl.ds(base + k * width + group + i, 1), :] * right
                    for i, t in enumerate(totals)
                )

            zero = jnp.zeros((cols, chan), F32)
            totals = lax.fori_loop(0, 2 * rows, step, (zero,) * min(6, count - group), unroll=4)
            for i, t in enumerate(totals):
                out_ref[group + i] = t.astype(out_ref.dtype)


def last_kernel(whole, upper, *refs):
    parts, (first_ref, gate_ref, final_ref, out_ref) = refs[:-4], refs[-4:]
    rows, cols, chan = first_ref.shape
    product = sum(ref[...].astype(F32) for ref in parts[:whole])
    top = sum(ref[...].astype(F32) for ref in parts[whole : whole + upper])
    low = sum(ref[...].astype(F32) for ref in parts[whole + upper :])
    product = product + jnp.concatenate([top, low], axis=0)
    mixed = layer_norm(product).astype(BF16).reshape(rows * cols, chan)
    update = jnp.dot(mixed, final_ref[...], preferred_element_type=F32)
    first = first_ref[...].astype(F32).reshape(rows * cols, chan)
    result = first + gate_ref[...].reshape(rows * cols, chan) * update
    out_ref[...] = result.astype(BF16).reshape(out_ref.shape)


def on_device(
    rows_n,
    cols_n,
    pair_rep,
    token_mask,
    out_project,
    out_gating,
    out_final,
    in_project,
    in_gating,
    in_final,
):
    rows, cols, chan = pair_rep.shape
    chips = rows_n // 2
    pieces = cols // (2 * rows)
    mask = token_mask.reshape(1, -1)
    block = shape((rows, cols, chan), BF16)
    block32 = shape((rows, cols, chan), F32)
    half = (rows, pieces * rows, chan)

    def along_row(v, bits):
        return lax.ppermute(v, "row", [(i, i ^ bits) for i in range(rows_n)])

    def shift(v, dx, core):
        pairs = [
            (r * cols_n + c, (r ^ core) * cols_n + (c ^ dx))
            for r in range(rows_n)
            for c in range(cols_n)
        ]
        return lax.ppermute(v, ("row", "col"), pairs)

    right = call(
        opening_kernel,
        block,
        [pltpu.with_memory_space_constraint(v, pltpu.HBM) for v in (pair_rep, mask, out_project)],
        scratch=[
            pltpu.VMEM(pair_rep.shape, BF16),
            pltpu.VMEM(mask.shape, jnp.int32),
            pltpu.VMEM((chan, out_project.shape[1] // 2), BF16),
            pltpu.SemaphoreType.DMA((3,)),
        ],
        flops=100_000_000,
        outside=(0, 1, 2),
    )
    rights = {0: right}
    bit = chips // 2
    while bit:
        for m in list(rights):
            rights[m | bit] = along_row(rights[m], 2 * bit)
        bit //= 2
    left, pair_copy = call(
        functools.partial(after, left_kernel, 1),
        [block, block],
        [right, pair_rep, mask, out_project],
        flops=100_000_000,
        outside=(0,),
    )
    pairs = [pair_copy] + [shift(pair_copy, dx, 0) for dx in range(1, cols_n)]
    core_left = along_row(left, 1)
    def product(blocks, sides, earlier=()):
        area = rows * len(blocks) * rows
        out = shape((area + sum(e.shape[0] for e in earlier[:1]), chan), BF16)
        return call(
            functools.partial(outgoing_kernel, len(earlier), len(sides)),
            [out] * len(sides),
            [*earlier, *sides] + [rights[m] for m in blocks],
            scratch=[
                pltpu.VMEM((cols * (-(-len(blocks) * rows // 8) * 8), chan), F32),
                pltpu.VMEM((rows * cols, chan), F32),
                pltpu.VMEM((area, chan), F32),
            ],
            flops=125_000_000 * len(blocks) * len(sides),
        )

    both = [left, core_left]
    early = []
    for h in range(cols_n - 1):
        early = product(range(h * pieces, (h + 1) * pieces), both, early)
    for m in range(chips - pieces, chips - 1):
        early = product([m], both, early)
    mine, other = early
    parts = [mine] + [shift(mine, dx, 0) for dx in range(1, cols_n)]
    exchanged = [parts + [shift(other, dx, 1) for dx in range(cols_n)]]
    (mine,) = product([chips - 1], [left])
    mine, core_left = lax.optimization_barrier((mine, core_left))
    (other,) = product([chips - 1], [core_left])
    other, out_gating = lax.optimization_barrier((other, out_gating))
    gates = call(
        functools.partial(gates_kernel, cols_n),
        [block, block32] * cols_n,
        pairs + [out_gating],
        flops=100_000_000,
    )
    gates = list(gates)
    other_core, gates[1] = lax.optimization_barrier((other, gates[1]))
    parts = [mine] + [shift(mine, dx, 0) for dx in range(1, cols_n)]
    parts += [shift(other_core, 0, 1)] + [shift(other, dx, 1) for dx in range(1, cols_n)]
    exchanged.append(parts)
    firsts, lefts = [], []
    for h in range(cols_n):
        area = rows * rows
        if h < cols_n - 1:
            groups, parts, earlier = [(h * pieces * area, 0, pieces)], exchanged[0], []
        else:
            groups = [((h * pieces + p) * area, p, 1) for p in range(pieces - 1)]
            groups.append((0, pieces - 1, 1))
            parts, earlier = exchanged[0] * (pieces - 1) + exchanged[1], firsts
        first, right, left_mine, left_other = call(
            functools.partial(first_kernel, cols_n, h, groups),
            [block, block, shape(half, BF16), shape(half, BF16)],
            parts + list(gates[2 * h : 2 * h + 2]) + [mask, out_final, in_project] + earlier,
            scratch=[
                pltpu.VMEM((rows * cols, chan), F32),
                pltpu.VMEM((rows * pieces * rows, chan), F32),
            ],
            flops=300_000_000,
        )
        firsts += [first, right]
        lefts.append([left_mine, along_row(left_other, 1)])

    core_right = along_row(right, 1)

    def partial_products(steps):
        used = lefts[steps[0][0] // pieces : steps[-1][0] // pieces + 1]
        wait = [] if used[-1] is lefts[-1] else lefts[-1]
        return call(
            functools.partial(after, functools.partial(incoming_kernel, steps), len(wait)),
            [shape((count, cols, chan), BF16 if m else F32) for m, _, count in steps],
            wait + [right, core_right] + sum(used, []),
            scratch=[
                pltpu.VMEM((2 * len(used) * rows * pieces * rows, chan), F32),
                pltpu.VMEM((2 * rows * cols, chan), F32),
            ],
            flops=20_000_000 * sum(count for *_, count in steps),
            outside=range(len(wait)),
        )

    cut = rows // 2
    top, low = [], []
    for h in range(1, cols_n):
        blocks = range(h * pieces, (h + 1) * pieces)
        relayed = partial_products([(m, cut, rows - cut) for m in blocks[1:]])
        relayed = [along_row(v, 2 * p) for p, v in enumerate(relayed, 1)]
        *direct, own = partial_products(
            [(m, 0, cut) for m in blocks] + [(blocks[0], cut, rows - cut)]
        )
        top += [along_row(v, 2 * m) for m, v in zip(blocks, direct)]
        total = sum((v.astype(F32) for v in relayed), own.astype(F32)).astype(BF16)
        low.append(along_row(total, 2 * blocks[0]))
    near = [partial_products([(m, 0, rows)])[0] for m in range(pieces)]
    near = [along_row(v, 2 * m) if m else v for m, v in enumerate(near)]
    gate = call(gate_kernel, block32, [first, in_gating], flops=50_000_000)
    return call(
        functools.partial(last_kernel, len(near), len(top)),
        block,
        near + top + low + [first, gate, in_final],
        flops=100_000_000,
    )


def solution(mesh):
    return jax.shard_map(
        functools.partial(on_device, mesh.shape["row"], mesh.shape["col"]),
        mesh=mesh,
        in_specs=(P(("groups", "row"), "col", None), P("groups"), P(), P(), P(), P(), P(), P()),
        out_specs=P(("groups", "row"), "col", None),
        check_vma=False,
    )
```

```python
import functools

import jax
import jax.numpy as jnp
from jax import lax
from jax.experimental import pallas as pl
from jax.experimental.pallas import tpu as pltpu
from jax.sharding import PartitionSpec as P

F32, BF16 = jnp.float32, jnp.bfloat16
VMEM = pl.BlockSpec(memory_space=pltpu.VMEM)
LIMIT = 40 * 1024 * 1024


def after(kernel, count, *refs):
    kernel(*refs[count:])


def call(kernel, outs, args, scratch=(), flops=10_000_000, outside=(), limit=LIMIT):
    single = not isinstance(outs, (list, tuple))
    outs = [outs] if single else list(outs)
    moved = sum(a.size * a.dtype.itemsize for a in args) + sum(
        o.size * o.dtype.itemsize for o in outs
    )
    result = pl.pallas_call(
        kernel,
        out_shape=outs,
        in_specs=[
            pl.BlockSpec(memory_space=pl.ANY) if n in outside else VMEM for n in range(len(args))
        ],
        out_specs=[VMEM] * len(outs),
        scratch_shapes=list(scratch),
        compiler_params=pltpu.CompilerParams(vmem_limit_bytes=limit),
        cost_estimate=pl.CostEstimate(flops=flops, bytes_accessed=moved, transcendentals=0),
    )(*args)
    return result[0] if single else result


def shape(dims, dtype):
    return jax.ShapeDtypeStruct(dims, dtype)


def sigmoid(v):
    return 0.5 * jnp.tanh(0.5 * v) + 0.5


def layer_norm(v):
    center = jnp.mean(v, axis=-1, keepdims=True)
    shifted = v - center
    spread = jnp.mean(shifted * shifted, axis=-1, keepdims=True)
    return shifted * lax.rsqrt(spread + 1e-05)


def place():
    row = lax.axis_index("row")
    return row // 2, row % 2, lax.axis_index("col")


def token_weights(mask_row, start, count):
    tokens = mask_row.shape[1]
    lane = lax.broadcasted_iota(jnp.int32, (count, tokens), 1)
    row = lax.broadcasted_iota(jnp.int32, (count, tokens), 0)
    hot = jnp.where(lane == row + start, mask_row, 0.0).astype(BF16)
    return jnp.dot(hot, jnp.ones((tokens, 128), BF16), preferred_element_type=F32)


def gated(normed, w, mask_ref, rows, cols, x):
    hidden = w.shape[1] // 2
    projected = jnp.dot(normed, w, preferred_element_type=F32)
    value = sigmoid(projected[:, hidden:]) * projected[:, :hidden]
    mask_row = mask_ref[...].astype(F32)
    row_w = token_weights(mask_row, lax.axis_index("row") * rows, -(-rows // 8) * 8)
    col_w = token_weights(mask_row, x * cols, cols)
    weights = row_w[:rows, None, :] * col_w[None, :, :]
    return value * weights.reshape(rows * cols, 128)


def normed_of(pair):
    rows, cols, chan = pair.shape
    return layer_norm(pair.astype(F32)).astype(BF16).reshape(rows * cols, chan)


def opening_kernel(pair_hbm, mask_hbm, w_hbm, right_ref, pair_ref, mask_scr, w_scr, sems):
    rows, cols, chan = pair_ref.shape
    width = w_scr.shape[1]
    copies = [
        pltpu.make_async_copy(pair_hbm, pair_ref, sems.at[0]),
        pltpu.make_async_copy(w_hbm.at[:, pl.ds(width, width)], w_scr, sems.at[1]),
        pltpu.make_async_copy(mask_hbm, mask_scr, sems.at[2]),
    ]
    for copy in copies:
        copy.start()
    for copy in copies:
        copy.wait()
    value = gated(
        normed_of(pair_ref[...]), w_scr[...], mask_scr, rows, cols, lax.axis_index("col")
    )
    right_ref[...] = value.astype(BF16).reshape(right_ref.shape)


def left_kernel(pair_ref, mask_ref, w_ref, left_ref, copy_ref):
    rows, cols, _ = pair_ref.shape
    w = w_ref[:, : w_ref.shape[1] // 2]
    value = gated(normed_of(pair_ref[...]), w, mask_ref, rows, cols, lax.axis_index("col"))
    left_ref[...] = value.astype(BF16).reshape(left_ref.shape)
    copy_ref[...] = pair_ref[...]


def gates_kernel(cols_n, *refs):
    pairs, w_ref, outs = refs[:cols_n], refs[cols_n], refs[cols_n + 1 :]
    rows, cols, _ = pairs[0].shape
    pieces = cols // (2 * rows)
    z, _, x = place()
    for h in range(cols_n):
        pair_ref, gate_ref = outs[2 * h : 2 * h + 2]
        for dx in range(cols_n):

            @pl.when(((z // pieces) ^ x ^ h) == dx)
            def _():
                pair_ref[...] = pairs[dx][...]

        gate = jnp.dot(normed_of(pair_ref[...]), w_ref[...], preferred_element_type=F32)
        gate_ref[...] = sigmoid(gate).reshape(gate_ref.shape)


def gate_kernel(pair_ref, w_ref, gate_ref):
    gate = jnp.dot(normed_of(pair_ref[...]), w_ref[...], preferred_element_type=F32)
    gate_ref[...] = sigmoid(gate).reshape(gate_ref.shape)


def outgoing_kernel(carried, sides, *refs):
    earlier, lefts, refs = refs[:carried], refs[carried : carried + sides], refs[carried + sides :]
    rights, outs, (r_scr, l_scr, o_scr) = refs[: -3 - sides], refs[-3 - sides : -3], refs[-3:]
    rows, cols, chan = lefts[0].shape
    blocks = len(rights)
    used = blocks * rows
    width = -(-used // 8) * 8
    z, _, _ = place()
    for m, ref in enumerate(rights):
        base = ((z % blocks) ^ m) * rows
        for j in range(rows):
            r_scr[pl.ds(base + j, cols, stride=width), :] = ref[j].astype(F32)
    for n, (left, out_ref) in enumerate(zip(lefts, outs)):
        l_scr[...] = left[...].astype(F32).reshape(rows * cols, chan)

        def step(block, totals):
            for u in range(16):
                k = block * 16 + u
                right = r_scr[pl.ds(pl.multiple_of(k * width, 8), width), :]
                totals = tuple(
                    t + l_scr[pl.ds(i * cols + k, 1), :] * right for i, t in enumerate(totals)
                )
            return totals

        zero = jnp.zeros((width, chan), F32)
        totals = lax.fori_loop(0, cols // 16, step, (zero,) * rows)
        for i, t in enumerate(totals):
            o_scr[pl.ds(i * used, used), :] = t[:used]
        begin = out_ref.shape[0] - rows * used
        if carried:
            out_ref[pl.ds(0, begin), :] = earlier[n][...]
        out_ref[pl.ds(begin, rows * used), :] = o_scr[...].astype(BF16)


def first_kernel(cols_n, h, groups, *refs):
    parts, refs = refs[: 2 * cols_n * len(groups)], refs[2 * cols_n * len(groups) :]
    pair_ref, gate_ref, mask_ref, final_ref, w_ref = refs[:5]
    earlier, refs = refs[5:-6], refs[-6:]
    first_ref, right_ref, mine_ref, other_ref, scr, half_scr = refs
    rows, cols, chan = pair_ref.shape
    pieces = cols // (2 * rows)
    z, core, x = place()
    for n, (begin, start, count) in enumerate(groups):
        group = parts[2 * cols_n * n : 2 * cols_n * (n + 1)]
        size = rows * count * rows
        for some, side in ((group[:cols_n], core), (group[cols_n:], 1 - core)):
            value = some[0][pl.ds(begin, size), :].astype(F32)
            for ref in some[1:]:
                value = value + ref[pl.ds(begin, size), :].astype(F32)
            half_scr[pl.ds(0, size), :] = value
            for i in range(rows):
                for p in range(count):
                    q = p if count == pieces else (z % pieces) ^ start
                    part = half_scr[pl.ds((i * count + p) * rows, rows), :]
                    scr[pl.ds(i * cols + (2 * q + side) * rows, rows), :] = part
    mixed = layer_norm(scr[...]).astype(BF16)
    update = jnp.dot(mixed, final_ref[...], preferred_element_type=F32)
    pair = pair_ref[...].astype(F32).reshape(rows * cols, chan)
    first = (pair + gate_ref[...].reshape(rows * cols, chan) * update).astype(BF16)
    first_ref[...] = first.reshape(first_ref.shape)
    normed = layer_norm(first.astype(F32)).astype(BF16)
    width = w_ref.shape[1] // 2
    block = (z // pieces) ^ h
    scr[...] = gated(normed, w_ref[:, :width], mask_ref, rows, cols, block)
    for out_ref, side in ((mine_ref, core), (other_ref, 1 - core)):
        for i in range(rows):
            for q in range(pieces):
                part = scr[pl.ds(i * cols + (2 * q + side) * rows, rows), :]
                half_scr[pl.ds((i * pieces + q) * rows, rows), :] = part
        half_block = half_scr[...].astype(BF16)
        if out_ref is other_ref and h == cols_n - 1:
            out_ref[pl.ds(rows, rows // 2)] = half_block.reshape(rows // 2, cols, chan)
        else:
            out_ref[...] = half_block.reshape(out_ref.shape)
    right = gated(normed, w_ref[:, width:], mask_ref, rows, cols, block)
    right_ref[...] = right.astype(BF16).reshape(right_ref.shape)
    for g in range(len(earlier) // 2):

        @pl.when(((z // pieces) ^ g) == x)
        def _():
            first_ref[...] = earlier[2 * g][...]
            right_ref[...] = earlier[2 * g + 1][...]

    if h == cols_n - 1:
        other_ref[pl.ds(0, rows)] = right_ref[...]


def incoming_kernel(steps, *refs):
    outs, (l_scr, r_scr) = refs[-2 - len(steps) : -2], refs[-2:]
    own_right, packed, *lefts = refs[: -2 - len(steps)]
    rows, cols, chan = own_right.shape
    width = lefts[0].shape[1]
    pieces = width // rows
    z, _, _ = place()
    for n, value in enumerate((own_right[...], packed[pl.ds(0, rows)])):
        r_scr[pl.ds(n * rows * cols, rows * cols), :] = value.astype(F32).reshape(-1, chan)
    lefts = [ref[...] for ref in lefts]
    if len(lefts) == 1:
        lefts.append(packed[pl.ds(rows, rows // 2)])
    for n, value in enumerate(lefts):
        l_scr[pl.ds(n * rows * width, rows * width), :] = value.astype(F32).reshape(-1, chan)
    for (m, begin, count), out_ref in zip(steps, outs):
        block = m // pieces - steps[0][0] // pieces
        base = block * (2 * rows * width) + ((z ^ m) % pieces) * rows + begin
        for group in range(0, count, 6):

            def step(k, totals):
                right = r_scr[pl.ds(pl.multiple_of(k * cols, 8), cols), :]
                return tuple(
                    t + l_scr[pl.ds(base + k * width + group + i, 1), :] * right
                    for i, t in enumerate(totals)
                )

            zero = jnp.zeros((cols, chan), F32)
            totals = lax.fori_loop(0, 2 * rows, step, (zero,) * min(6, count - group), unroll=12)
            for i, t in enumerate(totals):
                out_ref[group + i] = t.astype(out_ref.dtype)


def last_kernel(whole, upper, *refs):
    parts, (first_ref, gate_ref, final_ref, out_ref) = refs[:-4], refs[-4:]
    rows, cols, chan = first_ref.shape
    product = sum(ref[...].astype(F32) for ref in parts[:whole])
    top = sum(ref[...].astype(F32) for ref in parts[whole : whole + upper])
    low = sum(ref[...].astype(F32) for ref in parts[whole + upper :])
    product = product + jnp.concatenate([top, low], axis=0)
    mixed = layer_norm(product).astype(BF16).reshape(rows * cols, chan)
    update = jnp.dot(mixed, final_ref[...], preferred_element_type=F32)
    first = first_ref[...].astype(F32).reshape(rows * cols, chan)
    result = first + gate_ref[...].reshape(rows * cols, chan) * update
    out_ref[...] = result.astype(BF16).reshape(out_ref.shape)


def on_device(
    rows_n,
    cols_n,
    pair_rep,
    token_mask,
    out_project,
    out_gating,
    out_final,
    in_project,
    in_gating,
    in_final,
):
    rows, cols, chan = pair_rep.shape
    chips = rows_n // 2
    pieces = cols // (2 * rows)
    mask = token_mask.reshape(1, -1)
    block = shape((rows, cols, chan), BF16)
    block32 = shape((rows, cols, chan), F32)
    half = (rows, pieces * rows, chan)
    packed = (rows + rows // 2, cols, chan)

    def along_row(v, bits):
        return lax.ppermute(v, "row", [(i, i ^ bits) for i in range(rows_n)])

    def shift(v, dx, core):
        pairs = [
            (r * cols_n + c, (r ^ core) * cols_n + (c ^ dx))
            for r in range(rows_n)
            for c in range(cols_n)
        ]
        return lax.ppermute(v, ("row", "col"), pairs)

    right = call(
        opening_kernel,
        block,
        [pltpu.with_memory_space_constraint(v, pltpu.HBM) for v in (pair_rep, mask, out_project)],
        scratch=[
            pltpu.VMEM(pair_rep.shape, BF16),
            pltpu.VMEM(mask.shape, jnp.int32),
            pltpu.VMEM((chan, out_project.shape[1] // 2), BF16),
            pltpu.SemaphoreType.DMA((3,)),
        ],
        flops=100_000_000,
        outside=(0, 1, 2),
    )
    rights = {0: right}
    bit = chips // 2
    while bit:
        for m in list(rights):
            rights[m | bit] = along_row(rights[m], 2 * bit)
        bit //= 2
    left, pair_copy = call(
        functools.partial(after, left_kernel, 1),
        [block, block],
        [right, pair_rep, mask, out_project],
        flops=100_000_000,
        outside=(0,),
    )
    pairs = [pair_copy] + [shift(pair_copy, dx, 0) for dx in range(1, cols_n)]
    core_left = along_row(left, 1)
    def product(blocks, sides, earlier=()):
        area = rows * len(blocks) * rows
        out = shape((area + sum(e.shape[0] for e in earlier[:1]), chan), BF16)
        return call(
            functools.partial(outgoing_kernel, len(earlier), len(sides)),
            [out] * len(sides),
            [*earlier, *sides] + [rights[m] for m in blocks],
            scratch=[
                pltpu.VMEM((cols * (-(-len(blocks) * rows // 8) * 8), chan), F32),
                pltpu.VMEM((rows * cols, chan), F32),
                pltpu.VMEM((area, chan), F32),
            ],
            flops=125_000_000 * len(blocks) * len(sides),
        )

    both = [left, core_left]
    early = []
    for h in range(cols_n - 1):
        early = product(range(h * pieces, (h + 1) * pieces), both, early)
    for m in range(chips - pieces, chips - 1):
        early = product([m], both, early)
    mine, other = early
    parts = [mine] + [shift(mine, dx, 0) for dx in range(1, cols_n)]
    exchanged = [parts + [shift(other, dx, 1) for dx in range(cols_n)]]
    (mine,) = product([chips - 1], [left])
    mine, core_left = lax.optimization_barrier((mine, core_left))
    (other,) = product([chips - 1], [core_left])
    other, out_gating = lax.optimization_barrier((other, out_gating))
    gates = call(
        functools.partial(gates_kernel, cols_n),
        [block, block32] * cols_n,
        pairs + [out_gating],
        flops=100_000_000,
    )
    gates = list(gates)
    other_core, gates[1] = lax.optimization_barrier((other, gates[1]))
    parts = [mine] + [shift(mine, dx, 0) for dx in range(1, cols_n)]
    parts += [shift(other_core, 0, 1)] + [shift(other, dx, 1) for dx in range(1, cols_n)]
    exchanged.append(parts)
    firsts, lefts = [], []
    for h in range(cols_n):
        area = rows * rows
        if h < cols_n - 1:
            groups, parts, earlier = [(h * pieces * area, 0, pieces)], exchanged[0], []
        else:
            groups = [((h * pieces + p) * area, p, 1) for p in range(pieces - 1)]
            groups.append((0, pieces - 1, 1))
            parts, earlier = exchanged[0] * (pieces - 1) + exchanged[1], firsts
        first, right, left_mine, left_other = call(
            functools.partial(first_kernel, cols_n, h, groups),
            [block, block, shape(half, BF16), shape(half if h < cols_n - 1 else packed, BF16)],
            parts + list(gates[2 * h : 2 * h + 2]) + [mask, out_final, in_project] + earlier,
            scratch=[
                pltpu.VMEM((rows * cols, chan), F32),
                pltpu.VMEM((rows * pieces * rows, chan), F32),
            ],
            flops=300_000_000,
        )
        firsts += [first, right]
        arrived = along_row(left_other, 1)
        lefts.append([left_mine, arrived] if h < cols_n - 1 else [left_mine])

    def partial_products(steps):
        used = lefts[steps[0][0] // pieces : steps[-1][0] // pieces + 1]
        wait = []
        return call(
            functools.partial(after, functools.partial(incoming_kernel, steps), len(wait)),
            [shape((count, cols, chan), BF16 if m else F32) for m, _, count in steps],
            wait + [right, arrived] + sum(used, []),
            scratch=[
                pltpu.VMEM((2 * len(used) * rows * pieces * rows, chan), F32),
                pltpu.VMEM((2 * rows * cols, chan), F32),
            ],
            flops=20_000_000 * sum(count for *_, count in steps),
            outside=range(len(wait)),
        )

    cut = rows // 2
    top, low = [], []
    for h in range(1, cols_n):
        blocks = range(h * pieces, (h + 1) * pieces)
        relayed = partial_products([(m, cut, rows - cut) for m in blocks[1:]])
        relayed = [along_row(v, 2 * p) for p, v in enumerate(relayed, 1)]
        *direct, own = partial_products(
            [(m, 0, cut) for m in blocks] + [(blocks[0], cut, rows - cut)]
        )
        top += [along_row(v, 2 * m) for m, v in zip(blocks, direct)]
        total = sum((v.astype(F32) for v in relayed), own.astype(F32)).astype(BF16)
        low.append(along_row(total, 2 * blocks[0]))
    near = [partial_products([(m, 0, rows)])[0] for m in range(pieces)]
    near = [along_row(v, 2 * m) if m else v for m, v in enumerate(near)]
    gate = call(gate_kernel, block32, [first, in_gating], flops=50_000_000)
    return call(
        functools.partial(last_kernel, len(near), len(top)),
        block,
        near + top + low + [first, gate, in_final],
        flops=100_000_000,
    )


def solution(mesh):
    return jax.shard_map(
        functools.partial(on_device, mesh.shape["row"], mesh.shape["col"]),
        mesh=mesh,
        in_specs=(P(("groups", "row"), "col", None), P("groups"), P(), P(), P(), P(), P(), P()),
        out_specs=P(("groups", "row"), "col", None),
        check_vma=False,
    )
```

```python
import functools

import jax
import jax.numpy as jnp
from jax import lax
from jax.experimental import pallas as pl
from jax.experimental.pallas import tpu as pltpu
from jax.sharding import PartitionSpec as P

F32, BF16 = jnp.float32, jnp.bfloat16
VMEM = pl.BlockSpec(memory_space=pltpu.VMEM)
LIMIT = 40 * 1024 * 1024


def after(kernel, count, *refs):
    kernel(*refs[count:])


def call(kernel, outs, args, scratch=(), flops=10_000_000, outside=(), limit=LIMIT):
    single = not isinstance(outs, (list, tuple))
    outs = [outs] if single else list(outs)
    moved = sum(a.size * a.dtype.itemsize for a in args) + sum(
        o.size * o.dtype.itemsize for o in outs
    )
    result = pl.pallas_call(
        kernel,
        out_shape=outs,
        in_specs=[
            pl.BlockSpec(memory_space=pl.ANY) if n in outside else VMEM for n in range(len(args))
        ],
        out_specs=[VMEM] * len(outs),
        scratch_shapes=list(scratch),
        compiler_params=pltpu.CompilerParams(vmem_limit_bytes=limit),
        cost_estimate=pl.CostEstimate(flops=flops, bytes_accessed=moved, transcendentals=0),
    )(*args)
    return result[0] if single else result


def shape(dims, dtype):
    return jax.ShapeDtypeStruct(dims, dtype)


def sigmoid(v):
    return 0.5 * jnp.tanh(0.5 * v) + 0.5


def layer_norm(v):
    center = jnp.mean(v, axis=-1, keepdims=True)
    shifted = v - center
    spread = jnp.mean(shifted * shifted, axis=-1, keepdims=True)
    return shifted * lax.rsqrt(spread + 1e-05)


def place():
    row = lax.axis_index("row")
    return row // 2, row % 2, lax.axis_index("col")


def token_weights(mask_row, start, count):
    tokens = mask_row.shape[1]
    lane = lax.broadcasted_iota(jnp.int32, (count, tokens), 1)
    row = lax.broadcasted_iota(jnp.int32, (count, tokens), 0)
    hot = jnp.where(lane == row + start, mask_row, 0.0).astype(BF16)
    return jnp.dot(hot, jnp.ones((tokens, 128), BF16), preferred_element_type=F32)


def gated(normed, w, mask_ref, rows, cols, x):
    hidden = w.shape[1] // 2
    projected = jnp.dot(normed, w, preferred_element_type=F32)
    value = sigmoid(projected[:, hidden:]) * projected[:, :hidden]
    mask_row = mask_ref[...].astype(F32)
    row_w = token_weights(mask_row, lax.axis_index("row") * rows, -(-rows // 8) * 8)
    col_w = token_weights(mask_row, x * cols, cols)
    weights = row_w[:rows, None, :] * col_w[None, :, :]
    return value * weights.reshape(rows * cols, 128)


def normed_of(pair):
    rows, cols, chan = pair.shape
    return layer_norm(pair.astype(F32)).astype(BF16).reshape(rows * cols, chan)


def opening_kernel(pair_hbm, mask_hbm, w_hbm, right_ref, pair_ref, mask_scr, w_scr, sems):
    rows, cols, chan = pair_ref.shape
    width = w_scr.shape[1]
    copies = [
        pltpu.make_async_copy(pair_hbm, pair_ref, sems.at[0]),
        pltpu.make_async_copy(w_hbm.at[:, pl.ds(width, width)], w_scr, sems.at[1]),
        pltpu.make_async_copy(mask_hbm, mask_scr, sems.at[2]),
    ]
    for copy in copies:
        copy.start()
    for copy in copies:
        copy.wait()
    value = gated(
        normed_of(pair_ref[...]), w_scr[...], mask_scr, rows, cols, lax.axis_index("col")
    )
    right_ref[...] = value.astype(BF16).reshape(right_ref.shape)


def left_kernel(pair_ref, mask_ref, w_ref, left_ref, copy_ref):
    rows, cols, _ = pair_ref.shape
    w = w_ref[:, : w_ref.shape[1] // 2]
    value = gated(normed_of(pair_ref[...]), w, mask_ref, rows, cols, lax.axis_index("col"))
    left_ref[...] = value.astype(BF16).reshape(left_ref.shape)
    copy_ref[...] = pair_ref[...]


def gates_kernel(cols_n, *refs):
    pairs, w_ref, outs = refs[:cols_n], refs[cols_n], refs[cols_n + 1 :]
    rows, cols, _ = pairs[0].shape
    pieces = cols // (2 * rows)
    z, _, x = place()
    for h in range(cols_n):
        pair_ref, gate_ref = outs[2 * h : 2 * h + 2]
        for dx in range(cols_n):

            @pl.when(((z // pieces) ^ x ^ h) == dx)
            def _():
                pair_ref[...] = pairs[dx][...]

        gate = jnp.dot(normed_of(pair_ref[...]), w_ref[...], preferred_element_type=F32)
        gate_ref[...] = sigmoid(gate).reshape(gate_ref.shape)


def gate_kernel(pair_ref, w_ref, gate_ref):
    gate = jnp.dot(normed_of(pair_ref[...]), w_ref[...], preferred_element_type=F32)
    gate_ref[...] = sigmoid(gate).reshape(gate_ref.shape)


def outgoing_kernel(carried, sides, *refs):
    earlier, lefts, refs = refs[:carried], refs[carried : carried + sides], refs[carried + sides :]
    rights, outs, (r_scr, l_scr, o_scr) = refs[: -3 - sides], refs[-3 - sides : -3], refs[-3:]
    rows, cols, chan = lefts[0].shape
    blocks = len(rights)
    used = blocks * rows
    width = -(-used // 8) * 8
    z, _, _ = place()
    for m, ref in enumerate(rights):
        base = ((z % blocks) ^ m) * rows
        for j in range(rows):
            r_scr[pl.ds(base + j, cols, stride=width), :] = ref[j].astype(F32)
    for n, (left, out_ref) in enumerate(zip(lefts, outs)):
        l_scr[...] = left[...].astype(F32).reshape(rows * cols, chan)

        def step(block, totals):
            for u in range(16):
                k = block * 16 + u
                right = r_scr[pl.ds(pl.multiple_of(k * width, 8), width), :]
                totals = tuple(
                    t + l_scr[pl.ds(i * cols + k, 1), :] * right for i, t in enumerate(totals)
                )
            return totals

        zero = jnp.zeros((width, chan), F32)
        totals = lax.fori_loop(0, cols // 16, step, (zero,) * rows)
        for i, t in enumerate(totals):
            o_scr[pl.ds(i * used, used), :] = t[:used]
        begin = out_ref.shape[0] - rows * used
        if carried:
            out_ref[pl.ds(0, begin), :] = earlier[n][...]
        out_ref[pl.ds(begin, rows * used), :] = o_scr[...].astype(BF16)


def first_kernel(cols_n, h, groups, *refs):
    parts, refs = refs[: 2 * cols_n * len(groups)], refs[2 * cols_n * len(groups) :]
    pair_ref, gate_ref, mask_ref, final_ref, w_ref = refs[:5]
    earlier, refs = refs[5:-6], refs[-6:]
    first_ref, right_ref, mine_ref, other_ref, scr, half_scr = refs
    rows, cols, chan = pair_ref.shape
    pieces = cols // (2 * rows)
    z, core, x = place()
    for n, (begin, start, count) in enumerate(groups):
        group = parts[2 * cols_n * n : 2 * cols_n * (n + 1)]
        size = rows * count * rows
        for some, side in ((group[:cols_n], core), (group[cols_n:], 1 - core)):
            value = some[0][pl.ds(begin, size), :].astype(F32)
            for ref in some[1:]:
                value = value + ref[pl.ds(begin, size), :].astype(F32)
            half_scr[pl.ds(0, size), :] = value
            for i in range(rows):
                for p in range(count):
                    q = p if count == pieces else (z % pieces) ^ start
                    part = half_scr[pl.ds((i * count + p) * rows, rows), :]
                    scr[pl.ds(i * cols + (2 * q + side) * rows, rows), :] = part
    mixed = layer_norm(scr[...]).astype(BF16)
    update = jnp.dot(mixed, final_ref[...], preferred_element_type=F32)
    pair = pair_ref[...].astype(F32).reshape(rows * cols, chan)
    first = (pair + gate_ref[...].reshape(rows * cols, chan) * update).astype(BF16)
    first_ref[...] = first.reshape(first_ref.shape)
    normed = layer_norm(first.astype(F32)).astype(BF16)
    width = w_ref.shape[1] // 2
    block = (z // pieces) ^ h
    scr[...] = gated(normed, w_ref[:, :width], mask_ref, rows, cols, block)
    for out_ref, side in ((mine_ref, core), (other_ref, 1 - core)):
        for i in range(rows):
            for q in range(pieces):
                part = scr[pl.ds(i * cols + (2 * q + side) * rows, rows), :]
                half_scr[pl.ds((i * pieces + q) * rows, rows), :] = part
        half_block = half_scr[...].astype(BF16)
        if out_ref is other_ref and h == cols_n - 1:
            out_ref[pl.ds(rows, rows // 2)] = half_block.reshape(rows // 2, cols, chan)
        else:
            out_ref[...] = half_block.reshape(out_ref.shape)
    right = gated(normed, w_ref[:, width:], mask_ref, rows, cols, block)
    right_ref[...] = right.astype(BF16).reshape(right_ref.shape)
    for g in range(len(earlier) // 2):

        @pl.when(((z // pieces) ^ g) == x)
        def _():
            first_ref[...] = earlier[2 * g][...]
            right_ref[...] = earlier[2 * g + 1][...]

    if h == cols_n - 1:
        other_ref[pl.ds(0, rows)] = right_ref[...]


def incoming_kernel(steps, *refs):
    outs, (l_scr, r_scr) = refs[-2 - len(steps) : -2], refs[-2:]
    own_right, packed, *lefts = refs[: -2 - len(steps)]
    rows, cols, chan = own_right.shape
    width = lefts[0].shape[1]
    pieces = width // rows
    z, _, _ = place()
    for n, value in enumerate((own_right[...], packed[pl.ds(0, rows)])):
        r_scr[pl.ds(n * rows * cols, rows * cols), :] = value.astype(F32).reshape(-1, chan)
    lefts = [ref[...] for ref in lefts]
    if len(lefts) == 1:
        lefts.append(packed[pl.ds(rows, rows // 2)])
    for n, value in enumerate(lefts):
        l_scr[pl.ds(n * rows * width, rows * width), :] = value.astype(F32).reshape(-1, chan)
    for (m, begin, count), out_ref in zip(steps, outs):
        block = m // pieces - steps[0][0] // pieces
        base = block * (2 * rows * width) + ((z ^ m) % pieces) * rows + begin
        for group in range(0, count, 6):

            def step(k, totals):
                right = r_scr[pl.ds(pl.multiple_of(k * cols, 8), cols), :]
                return tuple(
                    t + l_scr[pl.ds(base + k * width + group + i, 1), :] * right
                    for i, t in enumerate(totals)
                )

            zero = jnp.zeros((cols, chan), F32)
            totals = lax.fori_loop(0, 2 * rows, step, (zero,) * min(6, count - group), unroll=24)
            for i, t in enumerate(totals):
                out_ref[group + i] = t.astype(out_ref.dtype)


def last_kernel(whole, upper, *refs):
    parts, (first_ref, gate_ref, final_ref, out_ref) = refs[:-4], refs[-4:]
    rows, cols, chan = first_ref.shape
    product = sum(ref[...].astype(F32) for ref in parts[:whole])
    top = sum(ref[...].astype(F32) for ref in parts[whole : whole + upper])
    low = sum(ref[...].astype(F32) for ref in parts[whole + upper :])
    product = product + jnp.concatenate([top, low], axis=0)
    mixed = layer_norm(product).astype(BF16).reshape(rows * cols, chan)
    update = jnp.dot(mixed, final_ref[...], preferred_element_type=F32)
    first = first_ref[...].astype(F32).reshape(rows * cols, chan)
    result = first + gate_ref[...].reshape(rows * cols, chan) * update
    out_ref[...] = result.astype(BF16).reshape(out_ref.shape)


def on_device(
    rows_n,
    cols_n,
    pair_rep,
    token_mask,
    out_project,
    out_gating,
    out_final,
    in_project,
    in_gating,
    in_final,
):
    rows, cols, chan = pair_rep.shape
    chips = rows_n // 2
    pieces = cols // (2 * rows)
    mask = token_mask.reshape(1, -1)
    block = shape((rows, cols, chan), BF16)
    block32 = shape((rows, cols, chan), F32)
    half = (rows, pieces * rows, chan)
    packed = (rows + rows // 2, cols, chan)

    def along_row(v, bits):
        return lax.ppermute(v, "row", [(i, i ^ bits) for i in range(rows_n)])

    def shift(v, dx, core):
        pairs = [
            (r * cols_n + c, (r ^ core) * cols_n + (c ^ dx))
            for r in range(rows_n)
            for c in range(cols_n)
        ]
        return lax.ppermute(v, ("row", "col"), pairs)

    right = call(
        opening_kernel,
        block,
        [pltpu.with_memory_space_constraint(v, pltpu.HBM) for v in (pair_rep, mask, out_project)],
        scratch=[
            pltpu.VMEM(pair_rep.shape, BF16),
            pltpu.VMEM(mask.shape, jnp.int32),
            pltpu.VMEM((chan, out_project.shape[1] // 2), BF16),
            pltpu.SemaphoreType.DMA((3,)),
        ],
        flops=100_000_000,
        outside=(0, 1, 2),
    )
    rights = {0: right}
    bit = chips // 2
    while bit:
        for m in list(rights):
            rights[m | bit] = along_row(rights[m], 2 * bit)
        bit //= 2
    left, pair_copy = call(
        functools.partial(after, left_kernel, 1),
        [block, block],
        [right, pair_rep, mask, out_project],
        flops=100_000_000,
        outside=(0,),
    )
    pairs = [pair_copy] + [shift(pair_copy, dx, 0) for dx in range(1, cols_n)]
    core_left = along_row(left, 1)
    def product(blocks, sides, earlier=()):
        area = rows * len(blocks) * rows
        out = shape((area + sum(e.shape[0] for e in earlier[:1]), chan), BF16)
        return call(
            functools.partial(outgoing_kernel, len(earlier), len(sides)),
            [out] * len(sides),
            [*earlier, *sides] + [rights[m] for m in blocks],
            scratch=[
                pltpu.VMEM((cols * (-(-len(blocks) * rows // 8) * 8), chan), F32),
                pltpu.VMEM((rows * cols, chan), F32),
                pltpu.VMEM((area, chan), F32),
            ],
            flops=125_000_000 * len(blocks) * len(sides),
        )

    both = [left, core_left]
    early = []
    for h in range(cols_n - 1):
        early = product(range(h * pieces, (h + 1) * pieces), both, early)
    for m in range(chips - pieces, chips - 1):
        early = product([m], both, early)
    mine, other = early
    parts = [mine] + [shift(mine, dx, 0) for dx in range(1, cols_n)]
    exchanged = [parts + [shift(other, dx, 1) for dx in range(cols_n)]]
    (mine,) = product([chips - 1], [left])
    mine, core_left = lax.optimization_barrier((mine, core_left))
    (other,) = product([chips - 1], [core_left])
    other, out_gating = lax.optimization_barrier((other, out_gating))
    gates = call(
        functools.partial(gates_kernel, cols_n),
        [block, block32] * cols_n,
        pairs + [out_gating],
        flops=100_000_000,
    )
    gates = list(gates)
    other_core, gates[1] = lax.optimization_barrier((other, gates[1]))
    parts = [mine] + [shift(mine, dx, 0) for dx in range(1, cols_n)]
    parts += [shift(other_core, 0, 1)] + [shift(other, dx, 1) for dx in range(1, cols_n)]
    exchanged.append(parts)
    firsts, lefts = [], []
    for h in range(cols_n):
        area = rows * rows
        if h < cols_n - 1:
            groups, parts, earlier = [(h * pieces * area, 0, pieces)], exchanged[0], []
        else:
            groups = [((h * pieces + p) * area, p, 1) for p in range(pieces - 1)]
            groups.append((0, pieces - 1, 1))
            parts, earlier = exchanged[0] * (pieces - 1) + exchanged[1], firsts
        first, right, left_mine, left_other = call(
            functools.partial(first_kernel, cols_n, h, groups),
            [block, block, shape(half, BF16), shape(half if h < cols_n - 1 else packed, BF16)],
            parts + list(gates[2 * h : 2 * h + 2]) + [mask, out_final, in_project] + earlier,
            scratch=[
                pltpu.VMEM((rows * cols, chan), F32),
                pltpu.VMEM((rows * pieces * rows, chan), F32),
            ],
            flops=300_000_000,
        )
        firsts += [first, right]
        arrived = along_row(left_other, 1)
        lefts.append([left_mine, arrived] if h < cols_n - 1 else [left_mine])

    def partial_products(steps):
        used = lefts[steps[0][0] // pieces : steps[-1][0] // pieces + 1]
        wait = []
        return call(
            functools.partial(after, functools.partial(incoming_kernel, steps), len(wait)),
            [shape((count, cols, chan), BF16 if m else F32) for m, _, count in steps],
            wait + [right, arrived] + sum(used, []),
            scratch=[
                pltpu.VMEM((2 * len(used) * rows * pieces * rows, chan), F32),
                pltpu.VMEM((2 * rows * cols, chan), F32),
            ],
            flops=20_000_000 * sum(count for *_, count in steps),
            outside=range(len(wait)),
        )

    cut = rows // 2
    top, low = [], []
    for h in range(1, cols_n):
        blocks = range(h * pieces, (h + 1) * pieces)
        relayed = partial_products([(m, cut, rows - cut) for m in blocks[1:]])
        relayed = [along_row(v, 2 * p) for p, v in enumerate(relayed, 1)]
        *direct, own = partial_products(
            [(m, 0, cut) for m in blocks] + [(blocks[0], cut, rows - cut)]
        )
        top += [along_row(v, 2 * m) for m, v in zip(blocks, direct)]
        total = sum((v.astype(F32) for v in relayed), own.astype(F32)).astype(BF16)
        low.append(along_row(total, 2 * blocks[0]))
    near = [partial_products([(m, 0, rows)])[0] for m in range(pieces)]
    near = [along_row(v, 2 * m) if m else v for m, v in enumerate(near)]
    gate = call(gate_kernel, block32, [first, in_gating], flops=50_000_000)
    return call(
        functools.partial(last_kernel, len(near), len(top)),
        block,
        near + top + low + [first, gate, in_final],
        flops=100_000_000,
    )


def solution(mesh):
    return jax.shard_map(
        functools.partial(on_device, mesh.shape["row"], mesh.shape["col"]),
        mesh=mesh,
        in_specs=(P(("groups", "row"), "col", None), P("groups"), P(), P(), P(), P(), P(), P()),
        out_specs=P(("groups", "row"), "col", None),
        check_vma=False,
    )
```
